256 devices in a mesh: dp: 32 (over z, x), fsdp: 8 (over y, core).
Axes of the slice: x: 4, y: 4, z: 8, core: 2. Of those that a mesh axis runs over, the one named last changes fastest.
Arguments:
- patches: bfloat16 [131072, 1152], P(('dp', 'fsdp')), may hold values from -6 to 6
- layer_norm_gain: float32 [1152], replicated, may hold values from 0.25 to 1.75
- layer_norm_bias: float32 [1152], replicated, may hold values from -3 to 3
- w_qkv: bfloat16 [1152, 1728], P('fsdp'), may hold values from -0.1875 to 0.1875
- qkv_bias: float32 [1728], replicated, may hold values from -3 to 3
- out_grad: bfloat16 [131072, 576], P(('dp', 'fsdp')), may hold values from -6 to 6
- lengths: int32 [512], P(('dp', 'fsdp')), may hold values from 1 to 256, as said below
- target: int32 [512], P(('dp', 'fsdp')), may hold values from 0 to 31, as said below
Outputs:
- attn_out: bfloat16 [131072, 576], P(('dp', 'fsdp'))
- patch_gradient: bfloat16 [131072, 1152], P(('dp', 'fsdp'))
- weight_grad: float32 [1152, 1728], P('fsdp')
- gain_gradient: float32 [1152], replicated
- bias_grad: float32 [1152], replicated
- qkv_bias_grad: float32 [1728], replicated
The draws below stay inside these ranges and needn't reach their ends.
Inputs may be any that keep to these rules, and one draw needn't show every extreme that they name: `target`: for each fsdp index and slot position s there is a number m, 0 <= m < 32, such that the slot of position s on dp index d goes to dp index d XOR m. `lengths`: every device holds a slot of 256 patches.
All inputs are finite; a program needn't handle non-finite values.
Results may differ from the reference program's by a relative error of at most 0.025.
Values may be sent and summed in bfloat16 or wider, within the bound.
A program may use at most 128 MiB of HBM per device.

```python
import jax
import jax.numpy as jnp
from jax import lax

D = 1152
HEADS = 8
HD = 72
SLOT = 256
SLOTS = 2
TOKENS = 131072
SLOT_COUNT = 512
N_DP = 32
N_FSDP = 8


def draw_lengths(key, part):
    key = jax.random.fold_in(key, 5)
    lowest = max(1, SLOT // 16)
    drawn = jax.random.randint(key, (N_DP * N_FSDP, SLOTS), lowest, SLOT + 1)
    drawn = drawn.at[:, 0].set(SLOT)
    return drawn.reshape(-1).astype(jnp.int32)


def draw_target(key, part):
    key = jax.random.fold_in(key, 11)
    masks = jax.random.randint(key, (N_FSDP, SLOTS), 0, N_DP).astype(jnp.int32)
    home = jnp.arange(N_DP, dtype=jnp.int32)[:, None, None]
    chosen = jnp.bitwise_xor(home, masks[None, :, :])
    return chosen.reshape(-1).astype(jnp.int32)


def levels(own_key, shape, pieces, low, top_value):
    loudness = 1.0
    for position, shards_of in pieces:
        heights = jax.random.uniform(jax.random.fold_in(jax.random.fold_in(own_key, 6), position), (shards_of,), jnp.float32, low / len(pieces), top_value / len(pieces))
        loudness = loudness * jnp.repeat(jnp.exp(heights), shape[position] // shards_of).reshape((-1,) + (1,) * (len(shape) - 1 - position))
    return loudness


def centred(key, shape, scale, bound, cuts=(), kind=jnp.bfloat16):
    gain = levels(key, shape, cuts, -0.22, 0.18) if cuts else 1.0
    values = jax.random.normal(key, shape, jnp.float32) * scale * gain
    return jnp.minimum(jnp.maximum(values, -bound), bound).astype(kind)


def setup_inputs(seed: int = 0) -> dict:
    arg_keys = jax.random.split(jax.random.key(seed), 9)
    return {
        "patches": centred(arg_keys[0], (TOKENS, D), 1.0, 6.0, ((0, 256),)),
        "layer_norm_gain": jnp.clip(1.0 + 0.15 * jax.random.normal(arg_keys[1], (D,), jnp.float32), 0.25, 1.75),
        "layer_norm_bias": centred(arg_keys[2], (D,), 0.5, 3.0, (), jnp.float32),
        "w_qkv": centred(arg_keys[3], (D, 3 * HEADS * HD), D ** -0.5, 0.1875, ((0, 8),)),
        "qkv_bias": centred(arg_keys[4], (3 * HEADS * HD,), 0.5, 3.0, (), jnp.float32),
        "out_grad": centred(arg_keys[5], (TOKENS, HEADS * HD), 1.0, 6.0, ((0, 256),)),
        "lengths": draw_lengths(jax.random.fold_in(arg_keys[8], 71), 0),
        "target": draw_target(jax.random.fold_in(arg_keys[8], 71), 0),
    }


def layer_statistics(patches):
    values = patches.astype(jnp.float32)
    center = values - lax.optimization_barrier(jnp.mean(values, axis=-1, keepdims=True))
    variance = lax.optimization_barrier(jnp.mean(center * center, axis=-1, keepdims=True))
    inverse_deviation = lax.rsqrt(variance + 1e-06)
    return (center * inverse_deviation, inverse_deviation)

def attend(qkv_slot, grad_slot, length):
    width = HEADS * HD
    count = qkv_slot.shape[0]
    query = qkv_slot[:, :width].reshape(count, HEADS, HD).astype(jnp.float32)
    keys = qkv_slot[:, width:2 * width].reshape(count, HEADS, HD).astype(jnp.float32)
    values = qkv_slot[:, 2 * width:].reshape(count, HEADS, HD).astype(jnp.float32)
    positions = jnp.arange(count, dtype=jnp.int32)
    live = positions < length
    score_scale = 1.0 / HD ** 0.5
    scores = jnp.einsum('qhd,khd->hqk', query, keys) * score_scale
    scores = jnp.where(live[None, None, :], scores, -1e+30)
    top = lax.optimization_barrier(jnp.max(scores, axis=-1, keepdims=True))
    weights = jnp.exp(scores - top) * live[None, None, :].astype(jnp.float32)
    probs = weights / lax.optimization_barrier(jnp.sum(weights, axis=-1, keepdims=True))
    rounded = probs.astype(jnp.bfloat16).astype(jnp.float32)
    output = jnp.einsum('hqk,khd->qhd', rounded, values)
    output = jnp.where(live[:, None, None], output, 0.0).astype(jnp.bfloat16).reshape(count, width)
    upstream = grad_slot.astype(jnp.float32).reshape(count, HEADS, HD)
    upstream = jnp.where(live[:, None, None], upstream, 0.0)
    grad_values = jnp.einsum('hqk,qhd->khd', rounded, upstream)
    grad_probs = jnp.einsum('qhd,khd->hqk', upstream, values)
    delta = lax.optimization_barrier(jnp.sum(grad_probs * probs, axis=-1, keepdims=True))
    grad_scores = (probs * (grad_probs - delta) * score_scale).astype(jnp.bfloat16).astype(jnp.float32)
    grad_query = jnp.einsum('hqk,khd->qhd', grad_scores, keys)
    grad_keys = jnp.einsum('hqk,qhd->khd', grad_scores, query)
    joined = jnp.concatenate([grad_query.reshape(count, width), grad_keys.reshape(count, width), grad_values.reshape(count, width)], axis=1)
    return (output, joined.astype(jnp.bfloat16))

def reference(patches, layer_norm_gain, layer_norm_bias, w_qkv, qkv_bias, out_grad, lengths, target):
    width = HEADS * HD
    slot_ids = jnp.arange(SLOT_COUNT, dtype=jnp.int32)
    blocks = slot_ids // SLOTS
    dest = (target * N_FSDP + blocks % N_FSDP) * SLOTS + slot_ids % SLOTS
    centered_scaled_input, inverse_deviation = layer_statistics(patches)
    normalized_input = (centered_scaled_input * layer_norm_gain + layer_norm_bias).astype(jnp.bfloat16)
    qkv = (jnp.dot(normalized_input, w_qkv, preferred_element_type=jnp.float32) + qkv_bias).astype(jnp.bfloat16)
    qkv_slots = qkv.reshape(SLOT_COUNT, SLOT, 3 * width)
    grad_slots = out_grad.reshape(SLOT_COUNT, SLOT, width)[dest]

    def one_slot(items):
        return attend(items[0], items[1], items[2])
    outputs, grads = lax.map(one_slot, (qkv_slots, grad_slots, lengths))
    attn_out = jnp.zeros((SLOT_COUNT, SLOT, width), jnp.bfloat16).at[dest].set(outputs).reshape(TOKENS, width)
    dqkv = grads.reshape(TOKENS, 3 * width)
    weight_grad = jnp.dot(normalized_input.T, dqkv, preferred_element_type=jnp.float32)
    qkv_bias_grad = lax.optimization_barrier(jnp.sum(dqkv.astype(jnp.float32), axis=0))
    normalized_gradient = jnp.dot(dqkv, w_qkv.T, preferred_element_type=jnp.float32).astype(jnp.bfloat16).astype(jnp.float32)
    gain_gradient = lax.optimization_barrier(jnp.sum(normalized_gradient * centered_scaled_input, axis=0))
    bias_grad = lax.optimization_barrier(jnp.sum(normalized_gradient, axis=0))
    scaled_input = normalized_gradient * layer_norm_gain
    patch_gradient = inverse_deviation * (scaled_input - lax.optimization_barrier(jnp.mean(scaled_input, axis=-1, keepdims=True)) - centered_scaled_input * lax.optimization_barrier(jnp.mean(scaled_input * centered_scaled_input, axis=-1, keepdims=True)))
    return (attn_out, patch_gradient.astype(jnp.bfloat16), weight_grad, gain_gradient, bias_grad, qkv_bias_grad)
```

```python
import jax
import jax.numpy as jnp
from jax import lax
from jax.experimental import pallas as pl
from jax.experimental.pallas import tpu as pltpu
from jax.sharding import PartitionSpec as P

HEADS = 8
HD = 72
WIDTH = HEADS * HD
SLOT = 256
NX, NZ, NY = 4, 8, 4
F32 = jnp.float32
BF16 = jnp.bfloat16
SCALE = 1.0 / HD**0.5

CHUNKS = [(0, 48), (48, 48), (96, 48), (144, 48), (192, 64)]
STEPS = ("z1", "x1", "z3", "x3", "z7")
ROUTE = [
    (slot, slot * SLOT + row, rows, tuple(STEPS[(i + k) % 5] for k in range(5)))
    for slot in range(2)
    for i, (row, rows) in enumerate(CHUNKS)
]
NC = len(ROUTE)
HALF_A = 80


def window(head):
    low = head * HD // 128 * 128
    return low, min((head * HD + HD + 127) // 128 * 128, WIDTH)


def nt(a, b):
    return lax.dot_general(a, b, (((1,), (1,)), ((), ())), preferred_element_type=F32)


def nn(a, b):
    return jnp.dot(a, b, preferred_element_type=F32)


def tn(a, b):
    return lax.dot_general(a, b, (((0,), (0,)), ((), ())), preferred_element_type=F32)


def kernel(
    len_ref,
    tgt_ref,
    x_ref,
    g_ref,
    b_ref,
    w_ref,
    qb_ref,
    og_ref,
    ao_ref,
    pg_ref,
    wg_ref,
    gg_ref,
    bg_ref,
    qg_ref,
    wf,
    xh,
    nrm,
    nrmt,
    rs,
    qkv,
    ks,
    probs,
    do,
    dqkv,
    o,
    s1,
    r1,
    s2,
    r2,
    part,
    rc,
    a1,
    b1,
    a2,
    b2,
    ta,
    tb,
    gsum,
    rx,
    xs,
    rz,
    full,
    vs,
    vr,
    vx,
    vz,
    route_sem,
    ag_sem,
    rs_sem,
    ar_sem,
    v_sem,
):
    dp = lax.axis_index("dp")
    fs = lax.axis_index("fsdp")
    z, x = dp // NX, dp % NX
    y, c = fs // 2, fs % 2
    partner = {
        "x1": z * NX + (x + 1 - 2 * (x % 2)),
        "x3": z * NX + (3 - x),
        "z1": (z + 1 - 2 * (z % 2)) * NX + x,
        "z3": ((z // 4) * 4 + 3 - z % 4) * NX + x,
        "z7": (7 - z) * NX + x,
    }
    y1, y2, y3 = y + 1 - 2 * (y % 2), (y + 2) % NY, 3 - y
    sib = (dp, y * 2 + 1 - c)
    at_y1 = (dp, y1 * 2 + c)
    at_y3 = (dp, y3 * 2 + c)
    at_x = [None] + [(z * NX + (x + j) % NX, fs) for j in range(1, NX)]
    at_z = [None] + [((z + j) % NZ * NX + x, fs) for j in range(1, NZ)]

    def remote(src, dst, send, recv, where):
        return pltpu.make_async_remote_copy(
            src_ref=src,
            dst_ref=dst,
            send_sem=send,
            recv_sem=recv,
            device_id=where,
            device_id_type=pl.DeviceIdType.MESH,
        )

    barrier = pltpu.get_barrier_semaphore()
    peers = [sib, at_y1, at_y3] + at_x[1:] + at_z[1:]
    for peer in peers:
        pl.semaphore_signal(barrier, inc=1, device_id=peer, device_id_type=pl.DeviceIdType.MESH)
    wf[pl.ds(fs * 144, 144), :] = w_ref[...]
    pl.semaphore_wait(barrier, len(peers))

    pending = []

    def start(copy):
        copy.start()
        pending.append(copy)
        return copy

    flip = []
    for slot in range(2):
        mask = jnp.bitwise_xor(tgt_ref[slot], dp)
        bits = [jnp.bitwise_and(jnp.right_shift(mask, i), 1) for i in range(5)]
        flip.append(
            {
                "x1": jnp.bitwise_xor(bits[0], bits[1]) == 1,
                "x3": bits[1] == 1,
                "z1": jnp.bitwise_xor(bits[2], bits[3]) == 1,
                "z3": jnp.bitwise_xor(bits[3], bits[4]) == 1,
                "z7": bits[4] == 1,
            }
        )

    def route(which, first, sbuf, rbuf, last):
        def source(i, k):
            _, row, rows, _ = ROUTE[i]
            ref = first if k == 0 else sbuf.at[k - 1]
            return ref.at[pl.ds(row, rows), :]

        copies = {}

        def send(i, k):
            _, row, rows, order = ROUTE[i]
            copies[i, k] = start(
                remote(
                    source(i, k),
                    rbuf.at[k, pl.ds(row, rows), :],
                    route_sem.at[which, 0, i, k],
                    route_sem.at[which, 1, i, k],
                    (partner[order[k]], fs),
                )
            )

        def advance(i, k):
            slot, row, rows, order = ROUTE[i]
            copies[i, k].wait_recv()
            value = jnp.where(
                flip[slot][order[k]], rbuf[k, pl.ds(row, rows), :], source(i, k)[...]
            )
            if k < 4:
                sbuf[k, pl.ds(row, rows), :] = value
                send(i, k + 1)
            else:
                last[pl.ds(row, rows), :] = value

        return send, advance

    send1, advance1 = route(0, og_ref, s1, r1, do)
    send2, advance2 = route(1, o, s2, r2, ao_ref)

    def ag(i, src, row, rows, where):
        return start(
            remote(src, wf.at[pl.ds(row, rows), :], ag_sem.at[0, i], ag_sem.at[1, i], where)
        )

    rest = 144 - HALF_A
    own = fs * 144
    row1, row2, row3 = (y1 * 2 + c) * 144, (y2 * 2 + c) * 144, (y3 * 2 + c) * 144
    head_rows, tail_rows = w_ref.at[pl.ds(0, HALF_A), :], w_ref.at[pl.ds(HALF_A, rest), :]

    def rows_of(row, rows):
        return wf.at[pl.ds(row, rows), :]

    ag_a0 = ag(0, head_rows, own, HALF_A, at_y1)
    ag_b0 = ag(1, tail_rows, own + HALF_A, rest, at_y3)
    for i in range(0, NC // 2):
        send1(i, 0)
        send1(i + NC // 2, 0)
    ag_a1 = ag(2, tail_rows, own + HALF_A, rest, at_y1)
    ag_b1 = ag(3, head_rows, own, HALF_A, at_y3)
    to_sib = [ag(4, w_ref, own, 144, sib)]

    def ag_relay():
        ag_a0.wait_recv()
        relay_a = ag(5, rows_of(row1, HALF_A), row1, HALF_A, at_y3)
        to_sib.append(ag(7, rows_of(row1, HALF_A), row1, HALF_A, sib))
        ag_b0.wait_recv()
        relay_b = ag(6, rows_of(row3 + HALF_A, rest), row3 + HALF_A, rest, at_y1)
        to_sib.append(ag(8, rows_of(row3 + HALF_A, rest), row3 + HALF_A, rest, sib))
        return relay_a, relay_b

    def ag_second():
        ag_a1.wait_recv()
        to_sib.append(ag(9, rows_of(row1 + HALF_A, rest), row1 + HALF_A, rest, sib))
        ag_b1.wait_recv()
        to_sib.append(ag(10, rows_of(row3, HALF_A), row3, HALF_A, sib))

    def ag_third(relays):
        relays[0].wait_recv()
        to_sib.append(ag(11, rows_of(row2, HALF_A), row2, HALF_A, sib))
        relays[1].wait_recv()
        to_sib.append(ag(12, rows_of(row2 + HALF_A, rest), row2 + HALF_A, rest, sib))
        for copy in to_sib:
            copy.wait_recv()

    def norm(slot):
        def step(i, _):
            rows = pl.ds(pl.multiple_of(slot * SLOT + i * 32, 32), 32)
            v = x_ref[rows, :].astype(F32)
            v = v - jnp.mean(v, axis=-1, keepdims=True)
            inv = lax.rsqrt(jnp.mean(v * v, axis=-1, keepdims=True) + 1e-6)
            v = v * inv
            xh[rows, :] = v
            rs[rows, :] = jnp.broadcast_to(inv, (32, 128))
            nrm[rows, :] = (v * g_ref[...] + b_ref[...]).astype(BF16)
            return 0

        lax.fori_loop(0, SLOT // 32, step, 0)

    def transpose():
        for slot in range(2):
            rows = slice(slot * SLOT, slot * SLOT + SLOT)
            nrmt[:, rows] = nrm[rows, :].T

    def project(slot):
        rows = slice(slot * SLOT, slot * SLOT + SLOT)
        qkv[rows, :] = (nn(nrm[rows, :], wf[...]) + qb_ref[...]).astype(BF16)
        ks[rows, :] = qkv[rows, WIDTH : 2 * WIDTH]

    def lanes(head):
        low, high = window(head)
        lane = lax.broadcasted_iota(jnp.int32, (1, high - low), 1) + low
        inside = (lane >= head * HD) & (lane < head * HD + HD)
        return inside.astype(F32).astype(BF16)

    def tiles_add(store, head, value):
        low, high = window(head)
        for t in range(low, high, 128):
            piece = value[:, t - low : min(t + 128, high) - low]
            store[t] = store[t] + piece if t in store else piece

    def forward(slot):
        rows = slice(slot * SLOT, slot * SLOT + SLOT)
        length = len_ref[slot]
        live_row = lax.broadcasted_iota(jnp.int32, (SLOT, 1), 0) < length
        out = {}
        for head in range(HEADS):
            low, high = window(head)
            mine = lanes(head)
            q = qkv[rows, low:high] * mine
            k = ks[rows, low:high]
            v = qkv[rows, 2 * WIDTH + low : 2 * WIDTH + high] * mine
            s = nt(k, q) * SCALE
            s = jnp.where(live_row, s, -1e30)
            e = jnp.exp(s - jnp.max(s, axis=0, keepdims=True))
            p = e / jnp.sum(e, axis=0, keepdims=True)
            probs[slot * HEADS + head] = p
            tiles_add(out, head, tn(p.astype(BF16), v).astype(BF16))
        for t, value in out.items():
            value = jnp.where(live_row, value.astype(F32), 0.0).astype(BF16)
            o[rows, t : t + value.shape[1]] = value

    def backward(slot, after):
        rows = slice(slot * SLOT, slot * SLOT + SLOT)
        length = len_ref[slot]
        live_row = lax.broadcasted_iota(jnp.int32, (SLOT, 1), 0) < length
        do[rows, :] = jnp.where(live_row, do[rows, :].astype(F32), 0.0).astype(BF16)
        gq, gk, gv = {}, {}, {}
        for head in range(HEADS):
            low, high = window(head)
            mine = lanes(head)
            q = qkv[rows, low:high] * mine
            k = ks[rows, low:high] * mine
            v = qkv[rows, 2 * WIDTH + low : 2 * WIDTH + high]
            up = do[rows, low:high] * mine
            p = probs[slot * HEADS + head]
            tiles_add(gv, head, nn(p.astype(BF16), up).astype(BF16))
            gp = nt(v, up)
            delta = jnp.sum(gp * p, axis=0, keepdims=True)
            gs = (p * (gp - delta) * SCALE).astype(BF16)
            tiles_add(gk, head, nn(gs, q).astype(BF16))
            tiles_add(gq, head, tn(gs, k).astype(BF16))
            after(slot, head)
        for t, value in gq.items():
            dqkv[rows, t : t + value.shape[1]] = value
        gk = jnp.concatenate([gk[t] for t in sorted(gk)], axis=1)
        dqkv[rows, WIDTH : 2 * WIDTH] = gk
        for t, value in gv.items():
            dqkv[rows, 2 * WIDTH + t : 2 * WIDTH + t + value.shape[1]] = value

    def weight_block(owner):
        return nn(nrmt[pl.ds(pl.multiple_of(owner * 144, 16), 144), :], dqkv[...])

    def put_block(par, j, value, extra):
        for t in range(14):
            piece = value[:, t * 128 : min(t * 128 + 128, 3 * WIDTH)]
            wide = piece.shape[1]
            if extra is not None:
                piece = piece + extra[j, pl.ds(t * 144, 144), 0:wide].astype(F32)
            part[par, j, pl.ds(t * 144, 144), 0:wide] = piece.astype(BF16)

    def rs_copy(i, src, dst, where):
        return remote(src, dst, rs_sem.at[0, i], rs_sem.at[1, i], where)

    def weights_for_sibling():
        def step(j, _):
            put_block(1 - c, j, weight_block(j * 2 + 1 - c), None)
            rs_copy(j, part.at[1 - c, j], rc.at[j], sib).start()
            return 0

        lax.fori_loop(0, NY, step, 0)

    def weights_own(order):
        out = {}
        for i, j in enumerate(order):
            rs_copy(j, part.at[1 - c, j], rc.at[j], sib).wait_recv()
            put_block(c, j, weight_block(j * 2 + c), rc)
            low, high = part.at[c, j, pl.ds(0, 1024), :], part.at[c, j, pl.ds(1024, 1024), :]
            if i == 0:
                out["a0"] = start(rs_copy(4, low, a1.at[0], at_y1))
                out["b0"] = start(rs_copy(5, high, b1.at[0], at_y3))
            elif i == 1:
                out["a1"] = start(rs_copy(6, low, a1.at[1], at_y1))
            elif i == 2:
                out["b1"] = start(rs_copy(7, high, b1.at[1], at_y3))
        return out

    def add(*terms):
        total = terms[0].astype(F32)
        for term in terms[1:]:
            total = total + term.astype(F32)
        return total

    def reduce_second(copies):
        copies["a0"].wait_recv()
        ta[...] = add(part[c, y3, pl.ds(0, 1024), :], a1[0]).astype(BF16)
        copies["a2"] = start(rs_copy(8, ta, a2, at_y3))
        copies["b0"].wait_recv()
        tb[...] = add(part[c, y1, pl.ds(1024, 1024), :], b1[0]).astype(BF16)
        copies["b2"] = start(rs_copy(9, tb, b2, at_y1))

    def reduce_last(copies):
        copies["a1"].wait_recv()
        copies["a2"].wait_recv()
        gsum[pl.ds(0, 1024), :] = add(part[c, y, pl.ds(0, 1024), :], a1[1], a2[...]).astype(BF16)
        copies["b1"].wait_recv()
        copies["b2"].wait_recv()
        gsum[pl.ds(1024, 1024), :] = add(part[c, y, pl.ds(1024, 1024), :], b1[1], b2[...]).astype(
            BF16
        )

    def ar_copy(i, src, dst, where):
        return start(remote(src, dst, ar_sem.at[0, i], ar_sem.at[1, i], where))

    def ar_x_send():
        return [
            ar_copy(j - 1, gsum.at[pl.ds((x + j) % NX * 512, 512), :], rx.at[j - 1], at_x[j])
            for j in range(1, NX)
        ]

    def ar_z_send(copies):
        for copy in copies:
            copy.wait_recv()
        xs[...] = add(gsum[pl.ds(x * 512, 512), :], rx[0], rx[1], rx[2]).astype(BF16)
        return [
            ar_copy(2 + j, xs.at[pl.ds((z + j) % NZ * 64, 64), :], rz.at[j - 1], at_z[j])
            for j in range(1, NZ)
        ]

    def ar_z_gather(copies):
        for copy in copies:
            copy.wait_recv()
        here = pl.ds(x * 512 + z * 64, 64)
        full[here, :] = add(xs[pl.ds(z * 64, 64), :], *[rz[j] for j in range(7)]).astype(BF16)
        return [ar_copy(9 + j, full.at[here, :], full.at[here, :], at_z[j]) for j in range(1, NZ)]

    def ar_x_gather(copies):
        for copy in copies:
            copy.wait_recv()
        here = pl.ds(x * 512, 512)
        return [ar_copy(16 + j, full.at[here, :], full.at[here, :], at_x[j]) for j in range(1, NX)]

    def v_copy(i, src, dst, where):
        return start(remote(src, dst, v_sem.at[0, i], v_sem.at[1, i], where))

    def v_pair(i, where):
        return v_copy(i, vs.at[i], vr.at[i], where)

    def v_next(i, copy):
        copy.wait_recv()
        vs[i + 1] = vs[i] + vr[i]

    def v_x_send():
        vx[x] = vs[3]
        return [v_copy(2 + j, vs.at[3], vx.at[x], at_x[j]) for j in range(1, NX)]

    def v_z_send(copies):
        for copy in copies:
            copy.wait_recv()
        total = vx[0] + vx[1] + vx[2] + vx[3]
        vs[4] = total
        vz[z] = total
        return [v_copy(5 + j, vs.at[4], vz.at[z], at_z[j]) for j in range(1, NZ)]

    def v_last(copies):
        for copy in copies:
            copy.wait_recv()
        total = vz[0]
        for j in range(1, NZ):
            total = total + vz[j]
        gg_ref[...] = total[:, 0:1152]
        bg_ref[...] = total[:, 1152:2304]
        qg_ref[...] = total[:, 2304:4032]

    def input_gradient():
        def step(i, carry):
            rows = pl.ds(pl.multiple_of(i * SLOT, SLOT), SLOT)
            probs_rows = nt(dqkv[rows, :], wf[...]).astype(BF16)
            nrm[rows, :] = probs_rows
            return carry

        lax.fori_loop(0, 2, step, 0)

        def piece(i, carry):
            gsum_, bsum_, qsum_ = carry
            rows = pl.ds(pl.multiple_of(i * 32, 32), 32)
            dn = nrm[rows, :].astype(F32)
            h = xh[rows, :]
            gsum_ = gsum_ + jnp.sum(dn * h, axis=0, keepdims=True)
            bsum_ = bsum_ + jnp.sum(dn, axis=0, keepdims=True)
            qsum_ = qsum_ + jnp.sum(dqkv[rows, :].astype(F32), axis=0, keepdims=True)
            d = dn * g_ref[...]
            m1 = jnp.mean(d, axis=-1, keepdims=True)
            m2 = jnp.mean(d * h, axis=-1, keepdims=True)
            pg_ref[rows, :] = (rs[rows, 0:1] * (d - m1 - h * m2)).astype(BF16)
            return gsum_, bsum_, qsum_

        zero = (jnp.zeros((1, 1152), F32), jnp.zeros((1, 1152), F32), jnp.zeros((1, 1728), F32))
        gsum_, bsum_, qsum_ = lax.fori_loop(0, 16, piece, zero)
        vs[0, :, 0:1152] = gsum_
        vs[0, :, 1152:2304] = bsum_
        vs[0, :, 2304:4032] = qsum_
        vs[0, :, 4032:4096] = jnp.zeros((1, 64), F32)

    def advance_all(advance, k):
        for i in range(NC // 2):
            advance(i, k)
            advance(i + NC // 2, k)

    for par in range(2):
        for j in range(NY):
            part[par, j, pl.ds(2016, 32), :] = jnp.zeros((32, 128), BF16)
            part[par, j, pl.ds(13 * 144, 144), :] = jnp.zeros((144, 128), BF16)
    norm(0)
    relays = ag_relay()
    norm(1)
    advance_all(advance1, 0)
    ag_second()
    transpose()
    advance_all(advance1, 1)
    ag_third(relays)
    project(0)
    advance_all(advance1, 2)
    project(1)
    forward(0)
    advance_all(advance1, 3)
    forward(1)
    advance_all(advance1, 4)
    for i in range(NC // 2):
        send2(i, 0)
        send2(i + NC // 2, 0)

    def after(slot, head):
        if slot == 1:
            for i in range(NC):
                if i * HEADS // NC == head:
                    advance2(i, 0)

    backward(0, after)
    backward(1, after)
    weights_for_sibling()
    for i in range(NC // 2):
        advance2(i, 1)
        advance2(i + NC // 2, 1)
    copies = weights_own((y2, y1, y3, y))
    input_gradient()
    va = v_pair(0, sib)
    advance_all(advance2, 2)
    v_next(0, va)
    va = v_pair(1, at_y1)
    reduce_second(copies)
    advance_all(advance2, 3)
    v_next(1, va)
    va = v_pair(2, at_y3)
    reduce_last(copies)
    ar = ar_x_send()
    v_next(2, va)
    vc = v_x_send()
    advance_all(advance2, 4)
    ar = ar_z_send(ar)
    vc = v_z_send(vc)
    ar = ar_z_gather(ar)
    ar = ar_x_gather(ar)
    v_last(vc)
    for copy in ar:
        copy.wait_recv()
    for t in range(14):
        wide = min(128, 3 * WIDTH - t * 128)
        wg_ref[:, t * 128 : t * 128 + wide] = full[pl.ds(t * 144, 144), 0:wide].astype(F32)
    for j in range(NY):
        rs_copy(j, part.at[1 - c, j], rc.at[j], sib).wait_send()
    for copy in pending:
        copy.wait_send()


def body(patches, layer_norm_gain, layer_norm_bias, w_qkv, qkv_bias, out_grad, lengths, target):
    rows, depth = patches.shape
    cols = w_qkv.shape[1]
    full_rows = 8 * w_qkv.shape[0]
    vmem = pl.BlockSpec(memory_space=pltpu.VMEM)
    smem = pl.BlockSpec(memory_space=pltpu.SMEM)
    shape = jax.ShapeDtypeStruct
    out = pl.pallas_call(
        kernel,
        out_shape=(
            shape((rows, WIDTH), BF16),
            shape((rows, depth), BF16),
            shape(w_qkv.shape, F32),
            shape((1, depth), F32),
            shape((1, depth), F32),
            shape((1, cols), F32),
        ),
        in_specs=[smem, smem] + [vmem] * 6,
        out_specs=[vmem] * 6,
        scratch_shapes=[
            pltpu.VMEM((full_rows, cols), BF16),
            pltpu.VMEM((rows, depth), F32),
            pltpu.VMEM((rows, depth), BF16),
            pltpu.VMEM((depth, rows), BF16),
            pltpu.VMEM((rows, 128), F32),
            pltpu.VMEM((rows, cols), BF16),
            pltpu.VMEM((rows, WIDTH), BF16),
            pltpu.VMEM((2 * HEADS, SLOT, SLOT), F32),
            pltpu.VMEM((rows, WIDTH), BF16),
            pltpu.VMEM((rows, cols), BF16),
            pltpu.VMEM((rows, WIDTH), BF16),
            pltpu.VMEM((4, rows, WIDTH), BF16),
            pltpu.VMEM((5, rows, WIDTH), BF16),
            pltpu.VMEM((4, rows, WIDTH), BF16),
            pltpu.VMEM((5, rows, WIDTH), BF16),
            pltpu.VMEM((2, NY, 2048, 128), BF16),
            pltpu.VMEM((NY, 2048, 128), BF16),
            pltpu.VMEM((2, 1024, 128), BF16),
            pltpu.VMEM((2, 1024, 128), BF16),
            pltpu.VMEM((1024, 128), BF16),
            pltpu.VMEM((1024, 128), BF16),
            pltpu.VMEM((1024, 128), BF16),
            pltpu.VMEM((1024, 128), BF16),
            pltpu.VMEM((2048, 128), BF16),
            pltpu.VMEM((3, 512, 128), BF16),
            pltpu.VMEM((512, 128), BF16),
            pltpu.VMEM((7, 64, 128), BF16),
            pltpu.VMEM((2048, 128), BF16),
            pltpu.VMEM((5, 1, 4096), F32),
            pltpu.VMEM((3, 1, 4096), F32),
            pltpu.VMEM((NX, 1, 4096), F32),
            pltpu.VMEM((NZ, 1, 4096), F32),
            pltpu.SemaphoreType.DMA((2, 2, NC, 5)),
            pltpu.SemaphoreType.DMA((2, 13)),
            pltpu.SemaphoreType.DMA((2, 10)),
            pltpu.SemaphoreType.DMA((2, 20)),
            pltpu.SemaphoreType.DMA((2, 13)),
        ],
        compiler_params=pltpu.CompilerParams(
            collective_id=0, has_side_effects=True, vmem_limit_bytes=58 * 1024 * 1024
        ),
    )(
        lengths,
        target,
        patches,
        layer_norm_gain[None],
        layer_norm_bias[None],
        w_qkv,
        qkv_bias[None],
        out_grad,
    )
    attn_out, patch_gradient, weight_grad, gain, bias, qbias = out
    return attn_out, patch_gradient, weight_grad, gain[0], bias[0], qbias[0]


def solution(mesh):
    return jax.shard_map(
        body,
        mesh=mesh,
        in_specs=(
            P(("dp", "fsdp"), None),
            P(),
            P(),
            P("fsdp", None),
            P(),
            P(("dp", "fsdp"), None),
            P(("dp", "fsdp")),
            P(("dp", "fsdp")),
        ),
        out_specs=(
            P(("dp", "fsdp"), None),
            P(("dp", "fsdp"), None),
            P("fsdp", None),
            P(),
            P(),
            P(),
        ),
        check_vma=False,
    )
```

```python
import jax
import jax.numpy as jnp
from jax import lax
from jax.experimental import pallas as pl
from jax.experimental.pallas import tpu as pltpu
from jax.sharding import PartitionSpec as P

HEADS = 8
HD = 72
WIDTH = HEADS * HD
SLOT = 256
NX, NZ, NY = 4, 8, 4
F32 = jnp.float32
BF16 = jnp.bfloat16
SCALE = 1.0 / HD**0.5

SWAPS = (
    (
        (-16711936, -16776961),
        (1717960704, -1717960705),
        (-65536, -1),
        (1717960704, -1717960705),
    ),
    (
        (1717960704, -1717960705),
        (-256, -1),
        (1717960704, -1717960705),
        (-16777216, -16776961),
    ),
)
CHUNK = WIDTH // 6


def chunk_steps(i):
    net = i % 2
    steps = [("z", net, s) for s in range(4)]
    first, second = (("x", 1), ("x", 3)) if i // 2 % 2 == 0 else (("x", 3), ("x", 1))
    at = i % 3
    steps.insert(at, first)
    steps.insert(at + 3, second)
    return tuple(steps)


ROUTE = [(slot, i * CHUNK, CHUNK, chunk_steps(i)) for slot in range(2) for i in range(6)]
HOPS = 6
NC = len(ROUTE)
HALF_A = 80


def window(head):
    low = head * HD // 128 * 128
    return low, min((head * HD + HD + 127) // 128 * 128, WIDTH)


def nt(a, b):
    return lax.dot_general(a, b, (((1,), (1,)), ((), ())), preferred_element_type=F32)


def nn(a, b):
    return jnp.dot(a, b, preferred_element_type=F32)


def tn(a, b):
    return lax.dot_general(a, b, (((0,), (0,)), ((), ())), preferred_element_type=F32)


def kernel(
    len_ref,
    tgt_ref,
    x_hbm,
    g_ref,
    b_ref,
    w_hbm,
    qb_ref,
    og_hbm,
    ao_hbm,
    pg_hbm,
    full,
    sums_ref,
    x_ref,
    og_ref,
    ao_ref,
    pg_ref,
    wf,
    xh,
    nrm,
    nrmt,
    rs,
    qkv,
    ks,
    probs,
    do,
    dqkv,
    o,
    s1,
    r1,
    s2,
    r2,
    part,
    rc,
    a1,
    b1,
    a2,
    b2,
    ta,
    tb,
    gsum,
    rx,
    xs,
    rz,
    vs,
    vr,
    vx,
    vz,
    route_sem,
    ag_sem,
    rs_sem,
    ar_sem,
    v_sem,
    io_sem,
):
    dp = lax.axis_index("dp")
    fs = lax.axis_index("fsdp")
    z, x = dp // NX, dp % NX
    y, c = fs // 2, fs % 2
    even = (z + 1 - 2 * (z % 2)) * NX + x
    odd = (z + NZ - 1 + 2 * (z % 2)) % NZ * NX + x
    partner = {("x", 1): z * NX + (x + 1 - 2 * (x % 2)), ("x", 3): z * NX + (3 - x)}
    for net in range(2):
        for stage in range(4):
            partner["z", net, stage] = odd if (net + stage) % 2 else even
    y1, y2, y3 = y + 1 - 2 * (y % 2), (y + 2) % NY, 3 - y
    sib = (dp, y * 2 + 1 - c)
    at_y1 = (dp, y1 * 2 + c)
    at_y3 = (dp, y3 * 2 + c)
    at_x = [None] + [(z * NX + (x + j) % NX, fs) for j in range(1, NX)]
    at_z = [None] + [((z + j) % NZ * NX + x, fs) for j in range(1, NZ)]

    def remote(src, dst, send, recv, where):
        return pltpu.make_async_remote_copy(
            src_ref=src,
            dst_ref=dst,
            send_sem=send,
            recv_sem=recv,
            device_id=where,
            device_id_type=pl.DeviceIdType.MESH,
        )

    load_og = pltpu.make_async_copy(og_hbm, og_ref, io_sem.at[0])
    load_w = pltpu.make_async_copy(w_hbm, wf.at[pl.ds(fs * 144, 144), :], io_sem.at[1])
    load_x = pltpu.make_async_copy(x_hbm, x_ref, io_sem.at[2])
    load_w.start()
    load_og.start()
    load_x.start()
    barrier = pltpu.get_barrier_semaphore()
    peers = [sib, at_y1, at_y3] + at_x[1:] + at_z[1:]
    for peer in peers:
        pl.semaphore_signal(barrier, inc=1, device_id=peer, device_id_type=pl.DeviceIdType.MESH)
    load_w.wait()
    load_og.wait()
    pl.semaphore_wait(barrier, len(peers))

    pending = []

    def start(copy):
        copy.start()
        pending.append(copy)
        return copy

    flip = []
    for slot in range(2):
        mask = jnp.bitwise_xor(tgt_ref[slot], dp)
        bits = [jnp.bitwise_and(jnp.right_shift(mask, i), 1) for i in range(2)]
        zmask = jnp.right_shift(mask, 2)
        shift = jnp.bitwise_and(zmask, 3) * 8 + z
        swap = {
            ("x", 1): jnp.bitwise_xor(bits[0], bits[1]) == 1,
            ("x", 3): bits[1] == 1,
        }
        for net in range(2):
            for stage in range(4):
                low, high = SWAPS[net][stage]
                word = jnp.where(zmask < 4, jnp.int32(low), jnp.int32(high))
                swap["z", net, stage] = jnp.bitwise_and(jnp.right_shift(word, shift), 1) == 1
        flip.append(swap)

    def route(which, first, sbuf, rbuf, last):
        def place(ref, i):
            slot, row, rows, _ = ROUTE[i]
            if len(ref.shape) == 2:
                return ref.at[pl.ds(row, rows), pl.ds(slot * SLOT, SLOT)]
            return ref.at[slot, pl.ds(row, rows), :]

        def source(i, k):
            return place(first if k == 0 else sbuf.at[k - 1], i)

        copies = {}

        def send(i, k):
            order = ROUTE[i][3]
            copies[i, k] = start(
                remote(
                    source(i, k),
                    place(rbuf.at[k], i),
                    route_sem.at[which, 0, i, k],
                    route_sem.at[which, 1, i, k],
                    (partner[order[k]], fs),
                )
            )

        def advance(i, k):
            slot, _, _, order = ROUTE[i]
            copies[i, k].wait_recv()
            value = jnp.where(
                flip[slot][order[k]], place(rbuf.at[k], i)[...], source(i, k)[...]
            )
            if k < HOPS - 1:
                place(sbuf.at[k], i)[...] = value
                send(i, k + 1)
            else:
                place(last, i)[...] = value

        return send, advance

    send1, advance1 = route(0, og_ref, s1, r1, do)
    send2, advance2 = route(1, o, s2, r2, ao_ref)

    def ag(i, src, row, rows, where):
        return start(
            remote(src, wf.at[pl.ds(row, rows), :], ag_sem.at[0, i], ag_sem.at[1, i], where)
        )

    rest = 144 - HALF_A
    own = fs * 144
    row1, row2, row3 = (y1 * 2 + c) * 144, (y2 * 2 + c) * 144, (y3 * 2 + c) * 144
    head_rows, tail_rows = wf.at[pl.ds(own, HALF_A), :], wf.at[pl.ds(own + HALF_A, rest), :]

    def rows_of(row, rows):
        return wf.at[pl.ds(row, rows), :]

    ag_a0 = ag(0, head_rows, own, HALF_A, at_y1)
    ag_b0 = ag(1, tail_rows, own + HALF_A, rest, at_y3)
    for i in range(NC):
        send1(i, 0)
    ag_a1 = ag(2, tail_rows, own + HALF_A, rest, at_y1)
    ag_b1 = ag(3, head_rows, own, HALF_A, at_y3)
    to_sib = [ag(4, wf.at[pl.ds(own, 144), :], own, 144, sib)]

    def ag_relay():
        ag_a0.wait_recv()
        relay_a = ag(5, rows_of(row1, HALF_A), row1, HALF_A, at_y3)
        to_sib.append(ag(7, rows_of(row1, HALF_A), row1, HALF_A, sib))
        ag_b0.wait_recv()
        relay_b = ag(6, rows_of(row3 + HALF_A, rest), row3 + HALF_A, rest, at_y1)
        to_sib.append(ag(8, rows_of(row3 + HALF_A, rest), row3 + HALF_A, rest, sib))
        return relay_a, relay_b

    def ag_second():
        ag_a1.wait_recv()
        to_sib.append(ag(9, rows_of(row1 + HALF_A, rest), row1 + HALF_A, rest, sib))
        ag_b1.wait_recv()
        to_sib.append(ag(10, rows_of(row3, HALF_A), row3, HALF_A, sib))

    def ag_third(relays):
        relays[0].wait_recv()
        to_sib.append(ag(11, rows_of(row2, HALF_A), row2, HALF_A, sib))
        relays[1].wait_recv()
        to_sib.append(ag(12, rows_of(row2 + HALF_A, rest), row2 + HALF_A, rest, sib))
        for copy in to_sib:
            copy.wait_recv()

    def norm(slot):
        def step(i, _):
            rows = pl.ds(pl.multiple_of(slot * SLOT + i * 32, 32), 32)
            v = x_ref[rows, :].astype(F32)
            v = v - jnp.mean(v, axis=-1, keepdims=True)
            inv = lax.rsqrt(jnp.mean(v * v, axis=-1, keepdims=True) + 1e-6)
            v = v * inv
            xh[rows, :] = v
            rs[rows, :] = jnp.broadcast_to(inv, (32, 128))
            nrm[rows, :] = (v * g_ref[...].reshape(1, -1) + b_ref[...].reshape(1, -1)).astype(BF16)
            return 0

        lax.fori_loop(0, SLOT // 32, step, 0)

    def transpose():
        for slot in range(2):
            rows = slice(slot * SLOT, slot * SLOT + SLOT)
            nrmt[:, rows] = nrm[rows, :].T

    def project(slot):
        rows = slice(slot * SLOT, slot * SLOT + SLOT)
        qkv[rows, :] = (nn(nrm[rows, :], wf[...]) + qb_ref[...].reshape(1, -1)).astype(BF16)
        ks[rows, :] = qkv[rows, WIDTH : 2 * WIDTH]

    def lanes(head):
        low, high = window(head)
        lane = lax.broadcasted_iota(jnp.int32, (1, high - low), 1) + low
        inside = (lane >= head * HD) & (lane < head * HD + HD)
        return inside.astype(F32).astype(BF16)

    def tiles_add(store, head, value, axis):
        low, high = window(head)
        for n in range(low, high, 128):
            piece = lax.slice_in_dim(value, n - low, min(n + 128, high) - low, axis=axis)
            store[n] = store[n] + piece if n in store else piece

    def forward(slot, after):
        rows = slice(slot * SLOT, slot * SLOT + SLOT)
        length = len_ref[slot]
        live = lax.broadcasted_iota(jnp.int32, (SLOT, 1), 0) < length
        live_lane = lax.broadcasted_iota(jnp.int32, (1, SLOT), 1) < length
        out = {}
        for head in range(HEADS):
            low, high = window(head)
            mine = lanes(head)
            q = qkv[rows, low:high] * mine
            k = ks[rows, low:high]
            v = qkv[rows, 2 * WIDTH + low : 2 * WIDTH + high] * mine
            s = jnp.where(live, nt(k, q) * SCALE, -1e30)
            e = jnp.exp(s - jnp.max(s, axis=0, keepdims=True))
            p = e / jnp.sum(e, axis=0, keepdims=True)
            probs[slot * HEADS + head] = p
            value = jnp.where(live_lane, tn(v, p.astype(BF16)), 0.0).astype(BF16)
            tiles_add(out, head, value, 0)
            after(head)
        for n, value in out.items():
            o[slot, n : n + value.shape[0], :] = value

    def backward(slot, after):
        rows = slice(slot * SLOT, slot * SLOT + SLOT)
        live_lane = lax.broadcasted_iota(jnp.int32, (1, SLOT), 1) < len_ref[slot]
        gq, gk, gv = {}, {}, {}
        for head in range(HEADS):
            low, high = window(head)
            mine = lanes(head)
            row = lax.broadcasted_iota(jnp.int32, (high - low, 1), 0) + low
            keep = (row >= head * HD) & (row < head * HD + HD) & live_lane
            q = qkv[rows, low:high] * mine
            k = ks[rows, low:high] * mine
            v = qkv[rows, 2 * WIDTH + low : 2 * WIDTH + high]
            up = jnp.where(keep, do[slot, low:high, :].astype(F32), 0.0).astype(BF16)
            p = probs[slot * HEADS + head]
            tiles_add(gv, head, nt(p.astype(BF16), up).astype(BF16), 1)
            gp = nn(v, up)
            delta = jnp.sum(gp * p, axis=0, keepdims=True)
            gs = (p * (gp - delta) * SCALE).astype(BF16)
            tiles_add(gk, head, nn(gs, q).astype(BF16), 1)
            tiles_add(gq, head, tn(gs, k).astype(BF16), 1)
            after(head)
        for n, value in gq.items():
            dqkv[rows, n : n + value.shape[1]] = value
        gk = jnp.concatenate([gk[n] for n in sorted(gk)], axis=1)
        dqkv[rows, WIDTH : 2 * WIDTH] = gk
        for n, value in gv.items():
            dqkv[rows, 2 * WIDTH + n : 2 * WIDTH + n + value.shape[1]] = value

    def weight_block(owner):
        return nn(nrmt[pl.ds(pl.multiple_of(owner * 144, 16), 144), :], dqkv[...])

    def put_block(par, j, value, extra):
        for t in range(14):
            piece = value[:, t * 128 : min(t * 128 + 128, 3 * WIDTH)]
            wide = piece.shape[1]
            if extra is not None:
                piece = piece + extra[j, pl.ds(t * 144, 144), 0:wide].astype(F32)
            part[par, j, pl.ds(t * 144, 144), 0:wide] = piece.astype(BF16)

    def rs_copy(i, src, dst, where):
        return remote(src, dst, rs_sem.at[0, i], rs_sem.at[1, i], where)

    def weights_for_sibling():
        def step(j, _):
            put_block(1 - c, j, weight_block(j * 2 + 1 - c), None)
            rs_copy(j, part.at[1 - c, j], rc.at[j], sib).start()
            return 0

        lax.fori_loop(0, NY, step, 0)

    def weights_own(order):
        out = {}
        for i, j in enumerate(order):
            rs_copy(j, part.at[1 - c, j], rc.at[j], sib).wait_recv()
            put_block(c, j, weight_block(j * 2 + c), rc)
            low, high = part.at[c, j, pl.ds(0, 1024), :], part.at[c, j, pl.ds(1024, 1024), :]
            if i == 0:
                out["a0"] = start(rs_copy(4, low, a1.at[0], at_y1))
                out["b0"] = start(rs_copy(5, high, b1.at[0], at_y3))
            elif i == 1:
                out["a1"] = start(rs_copy(6, low, a1.at[1], at_y1))
            elif i == 2:
                out["b1"] = start(rs_copy(7, high, b1.at[1], at_y3))
        return out

    def add(*terms):
        total = terms[0].astype(F32)
        for term in terms[1:]:
            total = total + term.astype(F32)
        return total

    def reduce_second(copies):
        copies["a0"].wait_recv()
        ta[...] = add(part[c, y3, pl.ds(0, 1024), :], a1[0]).astype(BF16)
        copies["a2"] = start(rs_copy(8, ta, a2, at_y3))
        copies["b0"].wait_recv()
        tb[...] = add(part[c, y1, pl.ds(1024, 1024), :], b1[0]).astype(BF16)
        copies["b2"] = start(rs_copy(9, tb, b2, at_y1))

    def reduce_last(copies):
        copies["a1"].wait_recv()
        copies["a2"].wait_recv()
        gsum[pl.ds(0, 1024), :] = add(part[c, y, pl.ds(0, 1024), :], a1[1], a2[...]).astype(BF16)
        copies["b1"].wait_recv()
        copies["b2"].wait_recv()
        gsum[pl.ds(1024, 1024), :] = add(part[c, y, pl.ds(1024, 1024), :], b1[1], b2[...]).astype(
            BF16
        )

    def ar_copy(i, src, dst, where):
        return start(remote(src, dst, ar_sem.at[0, i], ar_sem.at[1, i], where))

    def ar_x_send():
        return [
            ar_copy(j - 1, gsum.at[pl.ds((x + j) % NX * 512, 512), :], rx.at[j - 1], at_x[j])
            for j in range(1, NX)
        ]

    def ar_z_send(copies):
        for copy in copies:
            copy.wait_recv()
        xs[...] = add(gsum[pl.ds(x * 512, 512), :], rx[0], rx[1], rx[2]).astype(BF16)
        return [
            ar_copy(2 + j, xs.at[pl.ds((z + j) % NZ * 64, 64), :], rz.at[j - 1], at_z[j])
            for j in range(1, NZ)
        ]

    def ar_z_gather(copies):
        for copy in copies:
            copy.wait_recv()
        here = pl.ds(x * 512 + z * 64, 64)
        full[here, :] = add(xs[pl.ds(z * 64, 64), :], *[rz[j] for j in range(7)]).astype(BF16)
        return [ar_copy(9 + j, full.at[here, :], full.at[here, :], at_z[j]) for j in range(1, NZ)]

    def ar_x_gather(copies):
        for copy in copies:
            copy.wait_recv()
        here = pl.ds(x * 512, 512)
        return [ar_copy(16 + j, full.at[here, :], full.at[here, :], at_x[j]) for j in range(1, NX)]

    def v_copy(i, src, dst, where):
        return start(remote(src, dst, v_sem.at[0, i], v_sem.at[1, i], where))

    def v_pair(i, where):
        return v_copy(i, vs.at[i], vr.at[i], where)

    def v_next(i, copy):
        copy.wait_recv()
        vs[i + 1] = vs[i] + vr[i]

    def v_x_send():
        vx[x] = vs[3]
        return [v_copy(2 + j, vs.at[3], vx.at[x], at_x[j]) for j in range(1, NX)]

    def v_z_send(copies):
        for copy in copies:
            copy.wait_recv()
        total = vx[0] + vx[1] + vx[2] + vx[3]
        vs[4] = total
        vz[z] = total
        return [v_copy(5 + j, vs.at[4], vz.at[z], at_z[j]) for j in range(1, NZ)]

    def v_last(copies):
        for copy in copies:
            copy.wait_recv()
        total = vz[0]
        for j in range(1, NZ):
            total = total + vz[j]
        sums_ref[...] = total

    def input_gradient():
        def step(i, carry):
            rows = pl.ds(pl.multiple_of(i * SLOT, SLOT), SLOT)
            probs_rows = nt(dqkv[rows, :], wf[...]).astype(BF16)
            nrm[rows, :] = probs_rows
            return carry

        lax.fori_loop(0, 2, step, 0)

        def piece(i, carry):
            gsum_, bsum_, qsum_ = carry
            rows = pl.ds(pl.multiple_of(i * 32, 32), 32)
            dn = nrm[rows, :].astype(F32)
            h = xh[rows, :]
            gsum_ = gsum_ + jnp.sum(dn * h, axis=0, keepdims=True)
            bsum_ = bsum_ + jnp.sum(dn, axis=0, keepdims=True)
            qsum_ = qsum_ + jnp.sum(dqkv[rows, :].astype(F32), axis=0, keepdims=True)
            d = dn * g_ref[...].reshape(1, -1)
            m1 = jnp.mean(d, axis=-1, keepdims=True)
            m2 = jnp.mean(d * h, axis=-1, keepdims=True)
            pg_ref[rows, :] = (rs[rows, 0:1] * (d - m1 - h * m2)).astype(BF16)
            return gsum_, bsum_, qsum_

        zero = (jnp.zeros((1, 1152), F32), jnp.zeros((1, 1152), F32), jnp.zeros((1, 1728), F32))
        gsum_, bsum_, qsum_ = lax.fori_loop(0, 16, piece, zero)
        vs[0, :, 0:1152] = gsum_
        vs[0, :, 1152:2304] = bsum_
        vs[0, :, 2304:4032] = qsum_
        vs[0, :, 4032:4096] = jnp.zeros((1, 64), F32)

    def go(advance, slot, k):
        for i in range(NC // 2):
            advance(slot * (NC // 2) + i, k)

    def spread(events):
        events = list(events)

        def after(head):
            for event in events[head * len(events) // HEADS : (head + 1) * len(events) // HEADS]:
                event[0](*event[1:])

        return after

    def steps(advance, slot, k):
        return [(advance, slot * (NC // 2) + i, k) for i in range(NC // 2)]

    for par in range(2):
        for j in range(NY):
            part[par, j, pl.ds(2016, 32), :] = jnp.zeros((32, 128), BF16)
            part[par, j, pl.ds(13 * 144, 144), :] = jnp.zeros((144, 128), BF16)
    load_x.wait()
    norm(0)
    norm(1)
    go(advance1, 0, 0)
    relays = ag_relay()
    go(advance1, 1, 0)
    transpose()
    go(advance1, 0, 1)
    go(advance1, 1, 1)
    ag_second()
    go(advance1, 0, 2)
    go(advance1, 1, 2)
    go(advance1, 0, 3)
    go(advance1, 1, 3)
    ag_third(relays)
    project(0)
    go(advance1, 0, 4)
    go(advance1, 1, 4)
    project(1)
    forward(0, spread([]))
    for i in range(NC // 2):
        send2(i, 0)
    go(advance1, 0, 5)
    forward(1, spread([]))
    for i in range(NC // 2):
        send2(NC // 2 + i, 0)
    go(advance1, 1, 5)
    backward(0, spread(steps(advance2, 0, 0)))
    backward(1, spread(steps(advance2, 1, 0)))
    weights_for_sibling()
    go(advance2, 0, 1)
    go(advance2, 1, 1)
    copies = weights_own((y2, y1, y3, y))
    go(advance2, 0, 2)
    go(advance2, 1, 2)
    input_gradient()
    store_pg = pltpu.make_async_copy(pg_ref, pg_hbm, io_sem.at[0])
    store_pg.start()
    va = v_pair(0, sib)
    go(advance2, 0, 3)
    v_next(0, va)
    va = v_pair(1, at_y1)
    go(advance2, 1, 3)
    reduce_second(copies)
    v_next(1, va)
    va = v_pair(2, at_y3)
    go(advance2, 0, 4)
    go(advance2, 1, 4)
    reduce_last(copies)
    ar = ar_x_send()
    v_next(2, va)
    vc = v_x_send()
    store_ao = []
    for slot in range(2):
        go(advance2, slot, 5)
        copy = pltpu.make_async_copy(
            ao_ref.at[slot], ao_hbm.at[:, pl.ds(slot * SLOT, SLOT)], io_sem.at[1 + slot]
        )
        copy.start()
        store_ao.append(copy)
    ar = ar_z_send(ar)
    vc = v_z_send(vc)
    ar = ar_z_gather(ar)
    ar = ar_x_gather(ar)
    v_last(vc)
    for copy in ar:
        copy.wait_recv()
    for j in range(NY):
        rs_copy(j, part.at[1 - c, j], rc.at[j], sib).wait_send()
    for copy in pending:
        copy.wait_send()
    store_pg.wait()
    for copy in store_ao:
        copy.wait()


def finish(
    ao_in, pg_in, full, sums, ao_out, pg_out, wg_ref, gg_ref, bg_ref, qg_ref, ao, pg, in_sem, out_sem
):
    half = pg_in.shape[0] // 2
    pieces = [
        (ref_in.at[rows, :], ref.at[rows, :], ref_out.at[rows, :])
        for ref_in, ref, ref_out, rows in (
            (pg_in, pg, pg_out, pl.ds(0, half)),
            (pg_in, pg, pg_out, pl.ds(half, half)),
            (ao_in, ao, ao_out, pl.ds(0, WIDTH)),
        )
    ]
    loads = [
        pltpu.make_async_copy(src, mid, in_sem.at[i]) for i, (src, mid, _) in enumerate(pieces)
    ]
    stores = [
        pltpu.make_async_copy(mid, dst, out_sem.at[i]) for i, (_, mid, dst) in enumerate(pieces)
    ]
    for load in loads:
        load.start()
    for load, store in zip(loads, stores):
        load.wait()
        store.start()
    for t in range(14):
        wide = min(128, 3 * WIDTH - t * 128)
        wg_ref[:, t * 128 : t * 128 + wide] = full[pl.ds(t * 144, 144), 0:wide].astype(F32)
    gg_ref[...] = sums[0, 0:1152]
    bg_ref[...] = sums[0, 1152:2304]
    qg_ref[...] = sums[0, 2304:4032]
    for store in stores:
        store.wait()


def body(patches, layer_norm_gain, layer_norm_bias, w_qkv, qkv_bias, out_grad, lengths, target):
    rows, depth = patches.shape
    cols = w_qkv.shape[1]
    full_rows = 8 * w_qkv.shape[0]
    vmem = pl.BlockSpec(memory_space=pltpu.VMEM)
    smem = pl.BlockSpec(memory_space=pltpu.SMEM)
    hbm = pl.BlockSpec(memory_space=pl.ANY)
    shape = jax.ShapeDtypeStruct
    parts = pl.pallas_call(
        kernel,
        out_shape=(
            shape((WIDTH, rows), BF16),
            shape((rows, depth), BF16),
            shape((2048, 128), BF16),
            shape((1, 4096), F32),
        ),
        in_specs=[smem, smem, hbm, vmem, vmem, hbm, vmem, hbm],
        out_specs=[hbm, hbm, vmem, vmem],
        scratch_shapes=[
            pltpu.VMEM((rows, depth), BF16),
            pltpu.VMEM((WIDTH, rows), BF16),
            pltpu.VMEM((2, WIDTH, SLOT), BF16),
            pltpu.VMEM((rows, depth), BF16),
            pltpu.VMEM((full_rows, cols), BF16),
            pltpu.VMEM((rows, depth), F32),
            pltpu.VMEM((rows, depth), BF16),
            pltpu.VMEM((depth, rows), BF16),
            pltpu.VMEM((rows, 128), F32),
            pltpu.VMEM((rows, cols), BF16),
            pltpu.VMEM((rows, WIDTH), BF16),
            pltpu.VMEM((2 * HEADS, SLOT, SLOT), F32),
            pltpu.VMEM((2, WIDTH, SLOT), BF16),
            pltpu.VMEM((rows, cols), BF16),
            pltpu.VMEM((2, WIDTH, SLOT), BF16),
            pltpu.VMEM((5, 2, WIDTH, SLOT), BF16),
            pltpu.VMEM((6, 2, WIDTH, SLOT), BF16),
            pltpu.VMEM((5, 2, WIDTH, SLOT), BF16),
            pltpu.VMEM((6, 2, WIDTH, SLOT), BF16),
            pltpu.VMEM((2, NY, 2048, 128), BF16),
            pltpu.VMEM((NY, 2048, 128), BF16),
            pltpu.VMEM((2, 1024, 128), BF16),
            pltpu.VMEM((2, 1024, 128), BF16),
            pltpu.VMEM((1024, 128), BF16),
            pltpu.VMEM((1024, 128), BF16),
            pltpu.VMEM((1024, 128), BF16),
            pltpu.VMEM((1024, 128), BF16),
            pltpu.VMEM((2048, 128), BF16),
            pltpu.VMEM((3, 512, 128), BF16),
            pltpu.VMEM((512, 128), BF16),
            pltpu.VMEM((7, 64, 128), BF16),
            pltpu.VMEM((5, 1, 4096), F32),
            pltpu.VMEM((3, 1, 4096), F32),
            pltpu.VMEM((NX, 1, 4096), F32),
            pltpu.VMEM((NZ, 1, 4096), F32),
            pltpu.SemaphoreType.DMA((2, 2, NC, HOPS)),
            pltpu.SemaphoreType.DMA((2, 13)),
            pltpu.SemaphoreType.DMA((2, 10)),
            pltpu.SemaphoreType.DMA((2, 20)),
            pltpu.SemaphoreType.DMA((2, 13)),
            pltpu.SemaphoreType.DMA((3,)),
        ],
        compiler_params=pltpu.CompilerParams(
            collective_id=0, has_side_effects=True, vmem_limit_bytes=58 * 1024 * 1024
        ),
    )(
        lengths,
        target,
        patches,
        layer_norm_gain,
        layer_norm_bias,
        w_qkv,
        qkv_bias,
        out_grad.T,
    )
    out = pl.pallas_call(
        finish,
        out_shape=(
            shape((WIDTH, rows), BF16),
            shape((rows, depth), BF16),
            shape(w_qkv.shape, F32),
            shape((depth,), F32),
            shape((depth,), F32),
            shape((cols,), F32),
        ),
        in_specs=[hbm, hbm, vmem, vmem],
        out_specs=[hbm, hbm, vmem, vmem, vmem, vmem],
        scratch_shapes=[
            pltpu.VMEM((WIDTH, rows), BF16),
            pltpu.VMEM((rows, depth), BF16),
            pltpu.SemaphoreType.DMA((3,)),
            pltpu.SemaphoreType.DMA((3,)),
        ],
    )(*parts)
    attn_out, patch_gradient, weight_grad, gain, bias, qbias = out
    return attn_out.T, patch_gradient, weight_grad, gain, bias, qbias


def solution(mesh):
    return jax.shard_map(
        body,
        mesh=mesh,
        in_specs=(
            P(("dp", "fsdp"), None),
            P(),
            P(),
            P("fsdp", None),
            P(),
            P(("dp", "fsdp"), None),
            P(("dp", "fsdp")),
            P(("dp", "fsdp")),
        ),
        out_specs=(
            P(("dp", "fsdp"), None),
            P(("dp", "fsdp"), None),
            P("fsdp", None),
            P(),
            P(),
            P(),
        ),
        check_vma=False,
    )
```

```python
import jax
import jax.numpy as jnp
from jax import lax
from jax.experimental import pallas as pl
from jax.experimental.pallas import tpu as pltpu
from jax.sharding import PartitionSpec as P

HEADS = 8
HD = 72
WIDTH = HEADS * HD
SLOT = 256
NX, NZ, NY = 4, 8, 4
F32 = jnp.float32
BF16 = jnp.bfloat16
SCALE = 1.0 / HD**0.5

SWAPS = (
    (
        (-16711936, -16776961),
        (1717960704, -1717960705),
        (-65536, -1),
        (1717960704, -1717960705),
    ),
    (
        (1717960704, -1717960705),
        (-256, -1),
        (1717960704, -1717960705),
        (-16777216, -16776961),
    ),
)
CHUNK = WIDTH // 6


def chunk_steps(i):
    net = i % 2
    steps = [("z", net, s) for s in range(4)]
    first, second = (("x", 1), ("x", 3)) if i // 2 % 2 == 0 else (("x", 3), ("x", 1))
    at = i % 3
    steps.insert(at, first)
    steps.insert(at + 3, second)
    return tuple(steps)


ROUTE = [(slot, i * CHUNK, CHUNK, chunk_steps(i)) for slot in range(2) for i in range(6)]
HOPS = 6
NC = len(ROUTE)
HALF_A = 80
PIECES = 4
PIECE = 2048 // PIECES
HALF, QUARTER, SHARE = PIECE // 2, PIECE // NX, PIECE // NX // NZ


def window(head):
    low = head * HD // 128 * 128
    return low, min((head * HD + HD + 127) // 128 * 128, WIDTH)


def nt(a, b):
    return lax.dot_general(a, b, (((1,), (1,)), ((), ())), preferred_element_type=F32)


def nn(a, b):
    return jnp.dot(a, b, preferred_element_type=F32)


def tn(a, b):
    return lax.dot_general(a, b, (((0,), (0,)), ((), ())), preferred_element_type=F32)


def kernel(
    len_ref,
    tgt_ref,
    x_hbm,
    g_ref,
    b_ref,
    w_hbm,
    qb_ref,
    og_hbm,
    ao_hbm,
    pg_hbm,
    full,
    sums_ref,
    x_ref,
    og_ref,
    ao_ref,
    pg_ref,
    wf,
    xh,
    nrm,
    nrmt,
    rs,
    qkv,
    ks,
    probs,
    do,
    dqkv,
    o,
    s1,
    r1,
    s2,
    r2,
    part,
    rc,
    a1,
    b1,
    a2,
    b2,
    ta,
    tb,
    gsum,
    rx,
    xs,
    rz,
    vs,
    vr,
    vx,
    vz,
    route_sem,
    ag_sem,
    rs_sem,
    ar_sem,
    v_sem,
    io_sem,
):
    dp = lax.axis_index("dp")
    fs = lax.axis_index("fsdp")
    z, x = dp // NX, dp % NX
    y, c = fs // 2, fs % 2
    even = (z + 1 - 2 * (z % 2)) * NX + x
    odd = (z + NZ - 1 + 2 * (z % 2)) % NZ * NX + x
    partner = {("x", 1): z * NX + (x + 1 - 2 * (x % 2)), ("x", 3): z * NX + (3 - x)}
    for net in range(2):
        for stage in range(4):
            partner["z", net, stage] = odd if (net + stage) % 2 else even
    y1, y2, y3 = y + 1 - 2 * (y % 2), (y + 2) % NY, 3 - y
    sib = (dp, y * 2 + 1 - c)
    at_y1 = (dp, y1 * 2 + c)
    at_y3 = (dp, y3 * 2 + c)
    at_x = [None] + [(z * NX + (x + j) % NX, fs) for j in range(1, NX)]
    at_z = [None] + [((z + j) % NZ * NX + x, fs) for j in range(1, NZ)]

    def remote(src, dst, send, recv, where):
        return pltpu.make_async_remote_copy(
            src_ref=src,
            dst_ref=dst,
            send_sem=send,
            recv_sem=recv,
            device_id=where,
            device_id_type=pl.DeviceIdType.MESH,
        )

    load_og = pltpu.make_async_copy(og_hbm, og_ref, io_sem.at[0])
    load_w = pltpu.make_async_copy(w_hbm, wf.at[pl.ds(fs * 144, 144), :], io_sem.at[1])
    load_x = pltpu.make_async_copy(x_hbm, x_ref, io_sem.at[2])
    load_w.start()
    load_og.start()
    load_x.start()
    barrier = pltpu.get_barrier_semaphore()
    peers = [sib, at_y1, at_y3] + at_x[1:] + at_z[1:]
    for peer in peers:
        pl.semaphore_signal(barrier, inc=1, device_id=peer, device_id_type=pl.DeviceIdType.MESH)
    load_w.wait()
    load_og.wait()
    pl.semaphore_wait(barrier, len(peers))

    pending = []

    def start(copy):
        copy.start()
        pending.append(copy)
        return copy

    flip = []
    for slot in range(2):
        mask = jnp.bitwise_xor(tgt_ref[slot], dp)
        bits = [jnp.bitwise_and(jnp.right_shift(mask, i), 1) for i in range(2)]
        zmask = jnp.right_shift(mask, 2)
        shift = jnp.bitwise_and(zmask, 3) * 8 + z
        swap = {
            ("x", 1): jnp.bitwise_xor(bits[0], bits[1]) == 1,
            ("x", 3): bits[1] == 1,
        }
        for net in range(2):
            for stage in range(4):
                low, high = SWAPS[net][stage]
                word = jnp.where(zmask < 4, jnp.int32(low), jnp.int32(high))
                swap["z", net, stage] = jnp.bitwise_and(jnp.right_shift(word, shift), 1) == 1
        flip.append(swap)

    def route(which, first, sbuf, rbuf, last):
        def place(ref, i):
            slot, row, rows, _ = ROUTE[i]
            if len(ref.shape) == 2:
                return ref.at[pl.ds(row, rows), pl.ds(slot * SLOT, SLOT)]
            return ref.at[slot, pl.ds(row, rows), :]

        def source(i, k):
            return place(first if k == 0 else sbuf.at[k - 1], i)

        copies = {}

        def send(i, k):
            order = ROUTE[i][3]
            copies[i, k] = start(
                remote(
                    source(i, k),
                    place(rbuf.at[k], i),
                    route_sem.at[which, 0, i, k],
                    route_sem.at[which, 1, i, k],
                    (partner[order[k]], fs),
                )
            )

        def advance(i, k):
            slot, _, _, order = ROUTE[i]
            copies[i, k].wait_recv()
            value = jnp.where(
                flip[slot][order[k]], place(rbuf.at[k], i)[...], source(i, k)[...]
            )
            if k < HOPS - 1:
                place(sbuf.at[k], i)[...] = value
                send(i, k + 1)
            else:
                place(last, i)[...] = value

        return send, advance

    send1, advance1 = route(0, og_ref, s1, r1, do)
    send2, advance2 = route(1, o, s2, r2, ao_ref)

    def ag(i, src, row, rows, where):
        return start(
            remote(src, wf.at[pl.ds(row, rows), :], ag_sem.at[0, i], ag_sem.at[1, i], where)
        )

    rest = 144 - HALF_A
    own = fs * 144
    row1, row2, row3 = (y1 * 2 + c) * 144, (y2 * 2 + c) * 144, (y3 * 2 + c) * 144
    head_rows, tail_rows = wf.at[pl.ds(own, HALF_A), :], wf.at[pl.ds(own + HALF_A, rest), :]

    def rows_of(row, rows):
        return wf.at[pl.ds(row, rows), :]

    ag_a0 = ag(0, head_rows, own, HALF_A, at_y1)
    ag_b0 = ag(1, tail_rows, own + HALF_A, rest, at_y3)
    for i in range(NC):
        send1(i, 0)
    ag_a1 = ag(2, tail_rows, own + HALF_A, rest, at_y1)
    ag_b1 = ag(3, head_rows, own, HALF_A, at_y3)
    to_sib = [ag(4, wf.at[pl.ds(own, 144), :], own, 144, sib)]

    def ag_relay():
        ag_a0.wait_recv()
        relay_a = ag(5, rows_of(row1, HALF_A), row1, HALF_A, at_y3)
        to_sib.append(ag(7, rows_of(row1, HALF_A), row1, HALF_A, sib))
        ag_b0.wait_recv()
        relay_b = ag(6, rows_of(row3 + HALF_A, rest), row3 + HALF_A, rest, at_y1)
        to_sib.append(ag(8, rows_of(row3 + HALF_A, rest), row3 + HALF_A, rest, sib))
        return relay_a, relay_b

    def ag_second():
        ag_a1.wait_recv()
        to_sib.append(ag(9, rows_of(row1 + HALF_A, rest), row1 + HALF_A, rest, sib))
        ag_b1.wait_recv()
        to_sib.append(ag(10, rows_of(row3, HALF_A), row3, HALF_A, sib))

    def ag_third(relays):
        relays[0].wait_recv()
        to_sib.append(ag(11, rows_of(row2, HALF_A), row2, HALF_A, sib))
        relays[1].wait_recv()
        to_sib.append(ag(12, rows_of(row2 + HALF_A, rest), row2 + HALF_A, rest, sib))
        for copy in to_sib:
            copy.wait_recv()

    def norm(slot):
        def step(i, _):
            rows = pl.ds(pl.multiple_of(slot * SLOT + i * 32, 32), 32)
            v = x_ref[rows, :].astype(F32)
            v = v - jnp.mean(v, axis=-1, keepdims=True)
            inv = lax.rsqrt(jnp.mean(v * v, axis=-1, keepdims=True) + 1e-6)
            v = v * inv
            xh[rows, :] = v
            rs[rows, :] = jnp.broadcast_to(inv, (32, 128))
            nrm[rows, :] = (v * g_ref[...].reshape(1, -1) + b_ref[...].reshape(1, -1)).astype(BF16)
            return 0

        lax.fori_loop(0, SLOT // 32, step, 0)

    def transpose():
        for slot in range(2):
            rows = slice(slot * SLOT, slot * SLOT + SLOT)
            nrmt[:, rows] = nrm[rows, :].T

    def project(slot):
        rows = slice(slot * SLOT, slot * SLOT + SLOT)
        qkv[rows, :] = (nn(nrm[rows, :], wf[...]) + qb_ref[...].reshape(1, -1)).astype(BF16)
        ks[rows, :] = qkv[rows, WIDTH : 2 * WIDTH]

    def lanes(head):
        low, high = window(head)
        lane = lax.broadcasted_iota(jnp.int32, (1, high - low), 1) + low
        inside = (lane >= head * HD) & (lane < head * HD + HD)
        return inside.astype(F32).astype(BF16)

    def tiles_add(store, head, value, axis):
        low, high = window(head)
        for n in range(low, high, 128):
            piece = lax.slice_in_dim(value, n - low, min(n + 128, high) - low, axis=axis)
            store[n] = store[n] + piece if n in store else piece

    def forward(slot, after):
        rows = slice(slot * SLOT, slot * SLOT + SLOT)
        length = len_ref[slot]
        live = lax.broadcasted_iota(jnp.int32, (SLOT, 1), 0) < length
        live_lane = lax.broadcasted_iota(jnp.int32, (1, SLOT), 1) < length
        out = {}
        for head in range(HEADS):
            low, high = window(head)
            mine = lanes(head)
            q = qkv[rows, low:high] * mine
            k = ks[rows, low:high]
            v = qkv[rows, 2 * WIDTH + low : 2 * WIDTH + high] * mine
            s = jnp.where(live, nt(k, q) * SCALE, -1e30)
            e = jnp.exp(s - jnp.max(s, axis=0, keepdims=True))
            p = e / jnp.sum(e, axis=0, keepdims=True)
            probs[slot * HEADS + head] = p
            value = jnp.where(live_lane, tn(v, p.astype(BF16)), 0.0).astype(BF16)
            tiles_add(out, head, value, 0)
            after(head)
        for n, value in out.items():
            o[slot, n : n + value.shape[0], :] = value

    def backward(slot, after):
        rows = slice(slot * SLOT, slot * SLOT + SLOT)
        live_lane = lax.broadcasted_iota(jnp.int32, (1, SLOT), 1) < len_ref[slot]
        gq, gk, gv = {}, {}, {}
        for head in range(HEADS):
            low, high = window(head)
            mine = lanes(head)
            row = lax.broadcasted_iota(jnp.int32, (high - low, 1), 0) + low
            keep = (row >= head * HD) & (row < head * HD + HD) & live_lane
            q = qkv[rows, low:high] * mine
            k = ks[rows, low:high] * mine
            v = qkv[rows, 2 * WIDTH + low : 2 * WIDTH + high]
            up = jnp.where(keep, do[slot, low:high, :].astype(F32), 0.0).astype(BF16)
            p = probs[slot * HEADS + head]
            tiles_add(gv, head, nt(p.astype(BF16), up).astype(BF16), 1)
            gp = nn(v, up)
            delta = jnp.sum(gp * p, axis=0, keepdims=True)
            gs = (p * (gp - delta) * SCALE).astype(BF16)
            tiles_add(gk, head, nn(gs, q).astype(BF16), 1)
            tiles_add(gq, head, tn(gs, k).astype(BF16), 1)
            after(head)
        for n, value in gq.items():
            dqkv[rows, n : n + value.shape[1]] = value
        gk = jnp.concatenate([gk[n] for n in sorted(gk)], axis=1)
        dqkv[rows, WIDTH : 2 * WIDTH] = gk
        for n, value in gv.items():
            dqkv[rows, 2 * WIDTH + n : 2 * WIDTH + n + value.shape[1]] = value

    def weight_tiles(first, last):
        def step(pair, carry):
            cols = pl.ds(pl.multiple_of(pair * 256, 256), 256)
            value = nn(nrmt[...], dqkv[:, cols]).astype(BF16)
            for owner in range(8):
                for u in range(2):
                    row = pl.multiple_of(pair * 288 + u * 144, 16)
                    part[owner % 2, owner // 2, pl.ds(row, 144), :] = value[
                        owner * 144 : owner * 144 + 144, u * 128 : u * 128 + 128
                    ]
            return carry

        lax.fori_loop(first, last, step, 0)

    def rs_copy(p, i, src, dst, where):
        return start(remote(src, dst, rs_sem.at[0, p, i], rs_sem.at[1, p, i], where))

    def to_sibling(p):
        rows = pl.ds(p * PIECE, PIECE)
        return rs_copy(p, 0, part.at[1 - c, :, rows, :], rc.at[:, rows, :], sib)

    def add(*terms):
        total = terms[0].astype(F32)
        for term in terms[1:]:
            total = total + term.astype(F32)
        return total.astype(BF16)

    def reduce_first(p, core):
        core.wait_recv()
        rows, half = pl.ds(p * PIECE, PIECE), pl.ds(p * HALF, HALF)
        low, high = pl.ds(p * PIECE, HALF), pl.ds(p * PIECE + HALF, HALF)
        out = {}
        for i, j in enumerate((y2, y1, y3, y)):
            part[c, j, rows, :] = add(part[c, j, rows, :], rc[j, rows, :])
            if i == 0:
                out["a0"] = rs_copy(p, 1, part.at[c, j, low, :], a1.at[0, half, :], at_y1)
                out["b0"] = rs_copy(p, 2, part.at[c, j, high, :], b1.at[0, half, :], at_y3)
            elif i == 1:
                out["a1"] = rs_copy(p, 3, part.at[c, j, low, :], a1.at[1, half, :], at_y1)
            elif i == 2:
                out["b1"] = rs_copy(p, 4, part.at[c, j, high, :], b1.at[1, half, :], at_y3)
        return out

    def reduce_second(p, copies):
        half = pl.ds(p * HALF, HALF)
        low, high = pl.ds(p * PIECE, HALF), pl.ds(p * PIECE + HALF, HALF)
        copies["a0"].wait_recv()
        ta[half, :] = add(part[c, y3, low, :], a1[0, half, :])
        copies["a2"] = rs_copy(p, 5, ta.at[half, :], a2.at[half, :], at_y3)
        copies["b0"].wait_recv()
        tb[half, :] = add(part[c, y1, high, :], b1[0, half, :])
        copies["b2"] = rs_copy(p, 6, tb.at[half, :], b2.at[half, :], at_y1)

    def ar_copy(p, i, src, dst, where):
        return start(remote(src, dst, ar_sem.at[0, p, i], ar_sem.at[1, p, i], where))

    def wait_all(copies):
        for copy in copies:
            copy.wait_recv()

    def ar_x_send(p, copies):
        half = pl.ds(p * HALF, HALF)
        low, high = pl.ds(p * PIECE, HALF), pl.ds(p * PIECE + HALF, HALF)
        wait_all([copies["a1"], copies["a2"]])
        gsum[low, :] = add(part[c, y, low, :], a1[1, half, :], a2[half, :])
        wait_all([copies["b1"], copies["b2"]])
        gsum[high, :] = add(part[c, y, high, :], b1[1, half, :], b2[half, :])
        return [
            ar_copy(
                p,
                j - 1,
                gsum.at[pl.ds(p * PIECE + (x + j) % NX * QUARTER, QUARTER), :],
                rx.at[j - 1, pl.ds(p * QUARTER, QUARTER), :],
                at_x[j],
            )
            for j in range(1, NX)
        ]

    def ar_z_send(p, copies):
        wait_all(copies)
        here = pl.ds(p * QUARTER, QUARTER)
        xs[here, :] = add(
            gsum[pl.ds(p * PIECE + x * QUARTER, QUARTER), :], *[rx[j, here, :] for j in range(3)]
        )
        return [
            ar_copy(
                p,
                2 + j,
                xs.at[pl.ds(p * QUARTER + (z + j) % NZ * SHARE, SHARE), :],
                rz.at[j - 1, pl.ds(p * SHARE, SHARE), :],
                at_z[j],
            )
            for j in range(1, NZ)
        ]

    def ar_z_gather(p, copies):
        wait_all(copies)
        here = pl.ds(p * PIECE + x * QUARTER + z * SHARE, SHARE)
        full[here, :] = add(
            xs[pl.ds(p * QUARTER + z * SHARE, SHARE), :],
            *[rz[j, pl.ds(p * SHARE, SHARE), :] for j in range(7)],
        )
        return [
            ar_copy(p, 9 + j, full.at[here, :], full.at[here, :], at_z[j]) for j in range(1, NZ)
        ]

    def ar_x_gather(p, copies):
        wait_all(copies)
        here = pl.ds(p * PIECE + x * QUARTER, QUARTER)
        return [
            ar_copy(p, 16 + j, full.at[here, :], full.at[here, :], at_x[j]) for j in range(1, NX)
        ]

    def v_copy(i, src, dst, where):
        return start(remote(src, dst, v_sem.at[0, i], v_sem.at[1, i], where))

    def v_pair(i, where):
        return v_copy(i, vs.at[i], vr.at[i], where)

    def v_next(i, copy):
        copy.wait_recv()
        vs[i + 1] = vs[i] + vr[i]

    def v_x_send():
        vx[x] = vs[3]
        return [v_copy(2 + j, vs.at[3], vx.at[x], at_x[j]) for j in range(1, NX)]

    def v_z_send(copies):
        for copy in copies:
            copy.wait_recv()
        total = vx[0] + vx[1] + vx[2] + vx[3]
        vs[4] = total
        vz[z] = total
        return [v_copy(5 + j, vs.at[4], vz.at[z], at_z[j]) for j in range(1, NZ)]

    def v_last(copies):
        for copy in copies:
            copy.wait_recv()
        total = vz[0]
        for j in range(1, NZ):
            total = total + vz[j]
        sums_ref[...] = total

    def norm_gradient(slot):
        rows = slice(slot * SLOT, slot * SLOT + SLOT)
        nrm[rows, :] = nt(dqkv[rows, 0 : 3 * WIDTH], wf[...]).astype(BF16)

    def input_gradient(slot):
        def piece(i, carry):
            gsum_, bsum_, qsum_ = carry
            rows = pl.ds(pl.multiple_of(slot * SLOT + i * 32, 32), 32)
            dn = nrm[rows, :].astype(F32)
            h = xh[rows, :]
            gsum_ = gsum_ + jnp.sum(dn * h, axis=0, keepdims=True)
            bsum_ = bsum_ + jnp.sum(dn, axis=0, keepdims=True)
            qsum_ = qsum_ + jnp.sum(dqkv[rows, 0 : 3 * WIDTH].astype(F32), axis=0, keepdims=True)
            d = dn * g_ref[...].reshape(1, -1)
            m1 = jnp.mean(d, axis=-1, keepdims=True)
            m2 = jnp.mean(d * h, axis=-1, keepdims=True)
            pg_ref[rows, :] = (rs[rows, 0:1] * (d - m1 - h * m2)).astype(BF16)
            return gsum_, bsum_, qsum_

        zero = (jnp.zeros((1, 1152), F32), jnp.zeros((1, 1152), F32), jnp.zeros((1, 1728), F32))
        sums = lax.fori_loop(0, 8, piece, zero)
        for first, value in zip((0, 1152, 2304), sums):
            cols = slice(first, first + value.shape[1])
            vs[0, :, cols] = value if slot == 0 else vs[0, :, cols] + value
        if slot == 0:
            vs[0, :, 4032:4096] = jnp.zeros((1, 64), F32)

    def go(advance, slot, k):
        for i in range(NC // 2):
            advance(slot * (NC // 2) + i, k)

    def spread(events):
        events = list(events)

        def after(head):
            for event in events[head * len(events) // HEADS : (head + 1) * len(events) // HEADS]:
                event[0](*event[1:])

        return after

    def steps(advance, slot, k):
        return [(advance, slot * (NC // 2) + i, k) for i in range(NC // 2)]

    for par in range(2):
        for j in range(NY):
            part[par, j, pl.ds(2016, 32), :] = jnp.zeros((32, 128), BF16)
    dqkv[:, 3 * WIDTH :] = jnp.zeros((2 * SLOT, 64), BF16)
    load_x.wait()
    norm(0)
    norm(1)
    go(advance1, 0, 0)
    relays = ag_relay()
    go(advance1, 1, 0)
    transpose()
    go(advance1, 0, 1)
    go(advance1, 1, 1)
    ag_second()
    go(advance1, 0, 2)
    go(advance1, 1, 2)
    go(advance1, 0, 3)
    go(advance1, 1, 3)
    ag_third(relays)
    project(0)
    go(advance1, 0, 4)
    go(advance1, 1, 4)
    project(1)
    forward(0, spread([]))
    for i in range(NC // 2):
        send2(i, 0)
    go(advance1, 0, 5)
    forward(1, spread([]))
    for i in range(NC // 2):
        send2(NC // 2 + i, 0)
    go(advance1, 1, 5)
    backward(0, spread(steps(advance2, 0, 0)))
    backward(1, spread(steps(advance2, 1, 0)))
    core, moving = [], {}
    for p, (first, last) in enumerate(((0, 2), (2, 4), (4, 6), (6, 7))):
        weight_tiles(first, last)
        core.append(to_sibling(p))
        if p == 1:
            go(advance2, 0, 1)
    store_ao = []

    def stage(s, p):
        if s == 1:
            moving[p] = reduce_first(p, core[p])
        elif s == 2:
            reduce_second(p, moving[p])
        else:
            moving[p] = (ar_x_send, ar_z_send, ar_z_gather, ar_x_gather)[s - 3](p, moving[p])

    def store(slot):
        go(advance2, slot, 5)
        copy = pltpu.make_async_copy(
            ao_ref.at[slot], ao_hbm.at[:, pl.ds(slot * SLOT, SLOT)], io_sem.at[1 + slot]
        )
        copy.start()
        store_ao.append(copy)

    stage(1, 0)
    stage(1, 1)
    go(advance2, 1, 1)
    norm_gradient(0)
    go(advance2, 0, 2)
    stage(2, 0)
    stage(1, 2)
    go(advance2, 1, 2)
    input_gradient(0)
    stage(2, 1)
    stage(1, 3)
    go(advance2, 0, 3)
    stage(3, 0)
    norm_gradient(1)
    go(advance2, 1, 3)
    stage(2, 2)
    stage(3, 1)
    stage(4, 0)
    go(advance2, 0, 4)
    input_gradient(1)
    store_pg = pltpu.make_async_copy(pg_ref, pg_hbm, io_sem.at[0])
    store_pg.start()
    va = v_pair(0, sib)
    stage(2, 3)
    stage(3, 2)
    go(advance2, 1, 4)
    stage(4, 1)
    stage(5, 0)
    v_next(0, va)
    va = v_pair(1, at_y1)
    store(0)
    stage(3, 3)
    stage(4, 2)
    stage(5, 1)
    stage(6, 0)
    store(1)
    v_next(1, va)
    va = v_pair(2, at_y3)
    stage(4, 3)
    stage(5, 2)
    stage(6, 1)
    v_next(2, va)
    vc = v_x_send()
    stage(5, 3)
    stage(6, 2)
    vc = v_z_send(vc)
    stage(6, 3)
    v_last(vc)
    for p in range(PIECES):
        wait_all(moving[p])
    for copy in pending:
        copy.wait_send()
    store_pg.wait()
    for copy in store_ao:
        copy.wait()


def finish(
    ao_in, pg_in, full, sums, ao_out, pg_out, wg_ref, gg_ref, bg_ref, qg_ref, ao, pg, in_sem, out_sem
):
    half = pg_in.shape[0] // 2
    pieces = [
        (ref_in.at[rows, :], ref.at[rows, :], ref_out.at[rows, :])
        for ref_in, ref, ref_out, rows in (
            (pg_in, pg, pg_out, pl.ds(0, half)),
            (pg_in, pg, pg_out, pl.ds(half, half)),
            (ao_in, ao, ao_out, pl.ds(0, WIDTH)),
        )
    ]
    loads = [
        pltpu.make_async_copy(src, mid, in_sem.at[i]) for i, (src, mid, _) in enumerate(pieces)
    ]
    stores = [
        pltpu.make_async_copy(mid, dst, out_sem.at[i]) for i, (_, mid, dst) in enumerate(pieces)
    ]
    for load in loads:
        load.start()
    for load, store in zip(loads, stores):
        load.wait()
        store.start()
    for t in range(14):
        wide = min(128, 3 * WIDTH - t * 128)
        wg_ref[:, t * 128 : t * 128 + wide] = full[pl.ds(t * 144, 144), 0:wide].astype(F32)
    gg_ref[...] = sums[0, 0:1152]
    bg_ref[...] = sums[0, 1152:2304]
    qg_ref[...] = sums[0, 2304:4032]
    for store in stores:
        store.wait()


def body(patches, layer_norm_gain, layer_norm_bias, w_qkv, qkv_bias, out_grad, lengths, target):
    rows, depth = patches.shape
    cols = w_qkv.shape[1]
    full_rows = 8 * w_qkv.shape[0]
    vmem = pl.BlockSpec(memory_space=pltpu.VMEM)
    smem = pl.BlockSpec(memory_space=pltpu.SMEM)
    hbm = pl.BlockSpec(memory_space=pl.ANY)
    shape = jax.ShapeDtypeStruct
    parts = pl.pallas_call(
        kernel,
        out_shape=(
            shape((WIDTH, rows), BF16),
            shape((rows, depth), BF16),
            shape((2048, 128), BF16),
            shape((1, 4096), F32),
        ),
        in_specs=[smem, smem, hbm, vmem, vmem, hbm, vmem, hbm],
        out_specs=[hbm, hbm, vmem, vmem],
        scratch_shapes=[
            pltpu.VMEM((rows, depth), BF16),
            pltpu.VMEM((WIDTH, rows), BF16),
            pltpu.VMEM((2, WIDTH, SLOT), BF16),
            pltpu.VMEM((rows, depth), BF16),
            pltpu.VMEM((full_rows, cols), BF16),
            pltpu.VMEM((rows, depth), F32),
            pltpu.VMEM((rows, depth), BF16),
            pltpu.VMEM((depth, rows), BF16),
            pltpu.VMEM((rows, 128), F32),
            pltpu.VMEM((rows, cols), BF16),
            pltpu.VMEM((rows, WIDTH), BF16),
            pltpu.VMEM((2 * HEADS, SLOT, SLOT), F32),
            pltpu.VMEM((2, WIDTH, SLOT), BF16),
            pltpu.VMEM((rows, cols + 64), BF16),
            pltpu.VMEM((2, WIDTH, SLOT), BF16),
            pltpu.VMEM((5, 2, WIDTH, SLOT), BF16),
            pltpu.VMEM((6, 2, WIDTH, SLOT), BF16),
            pltpu.VMEM((5, 2, WIDTH, SLOT), BF16),
            pltpu.VMEM((6, 2, WIDTH, SLOT), BF16),
            pltpu.VMEM((2, NY, 2048, 128), BF16),
            pltpu.VMEM((NY, 2048, 128), BF16),
            pltpu.VMEM((2, 1024, 128), BF16),
            pltpu.VMEM((2, 1024, 128), BF16),
            pltpu.VMEM((1024, 128), BF16),
            pltpu.VMEM((1024, 128), BF16),
            pltpu.VMEM((1024, 128), BF16),
            pltpu.VMEM((1024, 128), BF16),
            pltpu.VMEM((2048, 128), BF16),
            pltpu.VMEM((3, 512, 128), BF16),
            pltpu.VMEM((512, 128), BF16),
            pltpu.VMEM((7, 64, 128), BF16),
            pltpu.VMEM((5, 1, 4096), F32),
            pltpu.VMEM((3, 1, 4096), F32),
            pltpu.VMEM((NX, 1, 4096), F32),
            pltpu.VMEM((NZ, 1, 4096), F32),
            pltpu.SemaphoreType.DMA((2, 2, NC, HOPS)),
            pltpu.SemaphoreType.DMA((2, 13)),
            pltpu.SemaphoreType.DMA((2, PIECES, 7)),
            pltpu.SemaphoreType.DMA((2, PIECES, 20)),
            pltpu.SemaphoreType.DMA((2, 13)),
            pltpu.SemaphoreType.DMA((3,)),
        ],
        compiler_params=pltpu.CompilerParams(
            collective_id=0, has_side_effects=True, vmem_limit_bytes=58 * 1024 * 1024
        ),
    )(
        lengths,
        target,
        patches,
        layer_norm_gain,
        layer_norm_bias,
        w_qkv,
        qkv_bias,
        out_grad.T,
    )
    out = pl.pallas_call(
        finish,
        out_shape=(
            shape((WIDTH, rows), BF16),
            shape((rows, depth), BF16),
            shape(w_qkv.shape, F32),
            shape((depth,), F32),
            shape((depth,), F32),
            shape((cols,), F32),
        ),
        in_specs=[hbm, hbm, vmem, vmem],
        out_specs=[hbm, hbm, vmem, vmem, vmem, vmem],
        scratch_shapes=[
            pltpu.VMEM((WIDTH, rows), BF16),
            pltpu.VMEM((rows, depth), BF16),
            pltpu.SemaphoreType.DMA((3,)),
            pltpu.SemaphoreType.DMA((3,)),
        ],
    )(*parts)
    attn_out, patch_gradient, weight_grad, gain, bias, qbias = out
    return attn_out.T, patch_gradient, weight_grad, gain, bias, qbias


def solution(mesh):
    return jax.shard_map(
        body,
        mesh=mesh,
        in_specs=(
            P(("dp", "fsdp"), None),
            P(),
            P(),
            P("fsdp", None),
            P(),
            P(("dp", "fsdp"), None),
            P(("dp", "fsdp")),
            P(("dp", "fsdp")),
        ),
        out_specs=(
            P(("dp", "fsdp"), None),
            P(("dp", "fsdp"), None),
            P("fsdp", None),
            P(),
            P(),
            P(),
        ),
        check_vma=False,
    )
```

```python
import jax
import jax.numpy as jnp
from jax import lax
from jax.experimental import pallas as pl
from jax.experimental.pallas import tpu as pltpu
from jax.sharding import PartitionSpec as P

HEADS = 8
HD = 72
WIDTH = HEADS * HD
SLOT = 256
NX, NZ, NY = 4, 8, 4
F32 = jnp.float32
BF16 = jnp.bfloat16
SCALE = 1.0 / HD**0.5

SWAPS = (
    (
        (-16711936, -16776961),
        (1717960704, -1717960705),
        (-65536, -1),
        (1717960704, -1717960705),
    ),
    (
        (1717960704, -1717960705),
        (-256, -1),
        (1717960704, -1717960705),
        (-16777216, -16776961),
    ),
)
CHUNK = WIDTH // 6


def chunk_steps(i):
    net = i % 2
    steps = [("z", net, s) for s in range(4)]
    first, second = (("x", 1), ("x", 3)) if i // 2 % 2 == 0 else (("x", 3), ("x", 1))
    at = i % 3
    steps.insert(at, first)
    steps.insert(at + 3, second)
    return tuple(steps)


ROUTE = [(slot, i * CHUNK, CHUNK, chunk_steps(i)) for slot in range(2) for i in range(6)]
HOPS = 6
NC = len(ROUTE)
HALF_A = 80
PIECES = 4
PIECE = 2048 // PIECES
HALF, QUARTER, SHARE = PIECE // 2, PIECE // NX, PIECE // NX // NZ


def window(head):
    low = head * HD // 128 * 128
    return low, min((head * HD + HD + 127) // 128 * 128, WIDTH)


def nt(a, b):
    return lax.dot_general(a, b, (((1,), (1,)), ((), ())), preferred_element_type=F32)


def nn(a, b):
    return jnp.dot(a, b, preferred_element_type=F32)


def tn(a, b):
    return lax.dot_general(a, b, (((0,), (0,)), ((), ())), preferred_element_type=F32)


def kernel(
    len_ref,
    tgt_ref,
    x_hbm,
    g_ref,
    b_ref,
    w_hbm,
    qb_ref,
    og_hbm,
    ao_hbm,
    pg_hbm,
    full,
    sums_ref,
    x_ref,
    og_ref,
    ao_ref,
    pg_ref,
    wf,
    xh,
    nrm,
    nrmt,
    rs,
    qkv,
    ks,
    probs,
    do,
    dqkv,
    o,
    s1,
    r1,
    s2,
    r2,
    part,
    rc,
    a1,
    b1,
    a2,
    b2,
    ta,
    tb,
    gsum,
    rx,
    xs,
    rz,
    vs,
    vr,
    vx,
    vz,
    route_sem,
    ag_sem,
    rs_sem,
    ar_sem,
    v_sem,
    io_sem,
):
    dp = lax.axis_index("dp")
    fs = lax.axis_index("fsdp")
    z, x = dp // NX, dp % NX
    y, c = fs // 2, fs % 2
    even = (z + 1 - 2 * (z % 2)) * NX + x
    odd = (z + NZ - 1 + 2 * (z % 2)) % NZ * NX + x
    partner = {("x", 1): z * NX + (x + 1 - 2 * (x % 2)), ("x", 3): z * NX + (3 - x)}
    for net in range(2):
        for stage in range(4):
            partner["z", net, stage] = odd if (net + stage) % 2 else even
    y1, y2, y3 = y + 1 - 2 * (y % 2), (y + 2) % NY, 3 - y
    sib = (dp, y * 2 + 1 - c)
    at_y1 = (dp, y1 * 2 + c)
    at_y3 = (dp, y3 * 2 + c)
    at_x = [None] + [(z * NX + (x + j) % NX, fs) for j in range(1, NX)]
    at_z = [None] + [((z + j) % NZ * NX + x, fs) for j in range(1, NZ)]

    def remote(src, dst, send, recv, where):
        return pltpu.make_async_remote_copy(
            src_ref=src,
            dst_ref=dst,
            send_sem=send,
            recv_sem=recv,
            device_id=where,
            device_id_type=pl.DeviceIdType.MESH,
        )

    load_og = pltpu.make_async_copy(og_hbm, og_ref, io_sem.at[0])
    load_w = pltpu.make_async_copy(w_hbm, wf.at[pl.ds(fs * 144, 144), :], io_sem.at[1])
    load_x = pltpu.make_async_copy(x_hbm, x_ref, io_sem.at[2])
    load_w.start()
    load_og.start()
    load_x.start()
    barrier = pltpu.get_barrier_semaphore()
    peers = [sib, at_y1, at_y3] + at_x[1:] + at_z[1:]
    for peer in peers:
        pl.semaphore_signal(barrier, inc=1, device_id=peer, device_id_type=pl.DeviceIdType.MESH)
    load_w.wait()
    load_og.wait()
    pl.semaphore_wait(barrier, len(peers))

    pending = []

    def start(copy):
        copy.start()
        pending.append(copy)
        return copy

    def drain(count):
        for copy in pending[:count]:
            copy.wait_send()
        del pending[:count]

    flip = []
    for slot in range(2):
        mask = jnp.bitwise_xor(tgt_ref[slot], dp)
        bits = [jnp.bitwise_and(jnp.right_shift(mask, i), 1) for i in range(2)]
        zmask = jnp.right_shift(mask, 2)
        shift = jnp.bitwise_and(zmask, 3) * 8 + z
        swap = {
            ("x", 1): jnp.bitwise_xor(bits[0], bits[1]) == 1,
            ("x", 3): bits[1] == 1,
        }
        for net in range(2):
            for stage in range(4):
                low, high = SWAPS[net][stage]
                word = jnp.where(zmask < 4, jnp.int32(low), jnp.int32(high))
                swap["z", net, stage] = jnp.bitwise_and(jnp.right_shift(word, shift), 1) == 1
        flip.append(swap)

    def route(which, first, sbuf, rbuf, last):
        def place(ref, i):
            slot, row, rows, _ = ROUTE[i]
            if len(ref.shape) == 2:
                return ref.at[pl.ds(row, rows), pl.ds(slot * SLOT, SLOT)]
            return ref.at[slot, pl.ds(row, rows), :]

        def source(i, k):
            return place(first if k == 0 else sbuf.at[k - 1], i)

        copies = {}

        def send(i, k):
            order = ROUTE[i][3]
            copies[i, k] = start(
                remote(
                    source(i, k),
                    place(rbuf.at[k], i),
                    route_sem.at[which, 0, i, k],
                    route_sem.at[which, 1, i, k],
                    (partner[order[k]], fs),
                )
            )

        def advance(i, k):
            slot, _, _, order = ROUTE[i]
            copies[i, k].wait_recv()
            value = jnp.where(
                flip[slot][order[k]], place(rbuf.at[k], i)[...], source(i, k)[...]
            )
            if k < HOPS - 1:
                place(sbuf.at[k], i)[...] = value
                send(i, k + 1)
            else:
                place(last, i)[...] = value

        return send, advance

    send1, advance1 = route(0, og_ref, s1, r1, do)
    send2, advance2 = route(1, o, s2, r2, ao_ref)

    def ag(i, src, row, rows, where):
        return start(
            remote(src, wf.at[pl.ds(row, rows), :], ag_sem.at[0, i], ag_sem.at[1, i], where)
        )

    rest = 144 - HALF_A
    own = fs * 144
    row1, row2, row3 = (y1 * 2 + c) * 144, (y2 * 2 + c) * 144, (y3 * 2 + c) * 144
    head_rows, tail_rows = wf.at[pl.ds(own, HALF_A), :], wf.at[pl.ds(own + HALF_A, rest), :]

    def rows_of(row, rows):
        return wf.at[pl.ds(row, rows), :]

    ag_a0 = ag(0, head_rows, own, HALF_A, at_y1)
    ag_b0 = ag(1, tail_rows, own + HALF_A, rest, at_y3)
    for i in range(NC):
        send1(i, 0)
    ag_a1 = ag(2, tail_rows, own + HALF_A, rest, at_y1)
    ag_b1 = ag(3, head_rows, own, HALF_A, at_y3)
    to_sib = [ag(4, wf.at[pl.ds(own, 144), :], own, 144, sib)]

    def ag_relay():
        ag_a0.wait_recv()
        relay_a = ag(5, rows_of(row1, HALF_A), row1, HALF_A, at_y3)
        to_sib.append(ag(7, rows_of(row1, HALF_A), row1, HALF_A, sib))
        ag_b0.wait_recv()
        relay_b = ag(6, rows_of(row3 + HALF_A, rest), row3 + HALF_A, rest, at_y1)
        to_sib.append(ag(8, rows_of(row3 + HALF_A, rest), row3 + HALF_A, rest, sib))
        return relay_a, relay_b

    def ag_second():
        ag_a1.wait_recv()
        to_sib.append(ag(9, rows_of(row1 + HALF_A, rest), row1 + HALF_A, rest, sib))
        ag_b1.wait_recv()
        to_sib.append(ag(10, rows_of(row3, HALF_A), row3, HALF_A, sib))

    def ag_third(relays):
        relays[0].wait_recv()
        to_sib.append(ag(11, rows_of(row2, HALF_A), row2, HALF_A, sib))
        relays[1].wait_recv()
        to_sib.append(ag(12, rows_of(row2 + HALF_A, rest), row2 + HALF_A, rest, sib))
        for copy in to_sib:
            copy.wait_recv()

    def norm(slot):
        def step(i, _):
            rows = pl.ds(pl.multiple_of(slot * SLOT + i * 32, 32), 32)
            v = x_ref[rows, :].astype(F32)
            v = v - jnp.mean(v, axis=-1, keepdims=True)
            inv = lax.rsqrt(jnp.mean(v * v, axis=-1, keepdims=True) + 1e-6)
            v = v * inv
            xh[rows, :] = v
            rs[rows, :] = jnp.broadcast_to(inv, (32, 128))
            nrm[rows, :] = (v * g_ref[...].reshape(1, -1) + b_ref[...].reshape(1, -1)).astype(BF16)
            return 0

        lax.fori_loop(0, SLOT // 32, step, 0)

    def transpose():
        for slot in range(2):
            rows = slice(slot * SLOT, slot * SLOT + SLOT)
            nrmt[:, rows] = nrm[rows, :].T

    def project(slot):
        rows = slice(slot * SLOT, slot * SLOT + SLOT)
        qkv[rows, :] = (nn(nrm[rows, :], wf[...]) + qb_ref[...].reshape(1, -1)).astype(BF16)
        ks[rows, :] = qkv[rows, WIDTH : 2 * WIDTH]

    def lanes(head):
        low, high = window(head)
        lane = lax.broadcasted_iota(jnp.int32, (1, high - low), 1) + low
        inside = (lane >= head * HD) & (lane < head * HD + HD)
        return inside.astype(F32).astype(BF16)

    def tiles_add(store, head, value, axis):
        low, high = window(head)
        for n in range(low, high, 128):
            piece = lax.slice_in_dim(value, n - low, min(n + 128, high) - low, axis=axis)
            store[n] = store[n] + piece if n in store else piece

    def forward(slot, after):
        rows = slice(slot * SLOT, slot * SLOT + SLOT)
        length = len_ref[slot]
        live = lax.broadcasted_iota(jnp.int32, (SLOT, 1), 0) < length
        live_lane = lax.broadcasted_iota(jnp.int32, (1, SLOT), 1) < length
        out = {}
        for head in range(HEADS):
            low, high = window(head)
            mine = lanes(head)
            q = qkv[rows, low:high] * mine
            k = ks[rows, low:high]
            v = qkv[rows, 2 * WIDTH + low : 2 * WIDTH + high] * mine
            s = jnp.where(live, nt(k, q) * SCALE, -1e30)
            e = jnp.exp(s - jnp.max(s, axis=0, keepdims=True))
            p = e / jnp.sum(e, axis=0, keepdims=True)
            probs[slot * HEADS + head] = p
            value = jnp.where(live_lane, tn(v, p.astype(BF16)), 0.0).astype(BF16)
            tiles_add(out, head, value, 0)
            after(head)
        for n, value in out.items():
            o[slot, n : n + value.shape[0], :] = value

    def backward(slot, after):
        rows = slice(slot * SLOT, slot * SLOT + SLOT)
        live_lane = lax.broadcasted_iota(jnp.int32, (1, SLOT), 1) < len_ref[slot]
        gq, gk, gv = {}, {}, {}
        for head in range(HEADS):
            low, high = window(head)
            mine = lanes(head)
            row = lax.broadcasted_iota(jnp.int32, (high - low, 1), 0) + low
            keep = (row >= head * HD) & (row < head * HD + HD) & live_lane
            q = qkv[rows, low:high] * mine
            k = ks[rows, low:high] * mine
            v = qkv[rows, 2 * WIDTH + low : 2 * WIDTH + high]
            up = jnp.where(keep, do[slot, low:high, :].astype(F32), 0.0).astype(BF16)
            p = probs[slot * HEADS + head]
            tiles_add(gv, head, nt(p.astype(BF16), up).astype(BF16), 1)
            gp = nn(v, up)
            delta = jnp.sum(gp * p, axis=0, keepdims=True)
            gs = (p * (gp - delta) * SCALE).astype(BF16)
            tiles_add(gk, head, nn(gs, q).astype(BF16), 1)
            tiles_add(gq, head, tn(gs, k).astype(BF16), 1)
            after(head)
        for n, value in gq.items():
            dqkv[rows, n : n + value.shape[1]] = value
        gk = jnp.concatenate([gk[n] for n in sorted(gk)], axis=1)
        dqkv[rows, WIDTH : 2 * WIDTH] = gk
        for n, value in gv.items():
            dqkv[rows, 2 * WIDTH + n : 2 * WIDTH + n + value.shape[1]] = value

    def weight_tiles(first, last):
        def step(pair, carry):
            cols = pl.ds(pl.multiple_of(pair * 256, 256), 256)
            value = nn(nrmt[...], dqkv[:, cols]).astype(BF16)
            for owner in range(8):
                for u in range(2):
                    row = pl.multiple_of(pair * 288 + u * 144, 16)
                    part[owner % 2, owner // 2, pl.ds(row, 144), :] = value[
                        owner * 144 : owner * 144 + 144, u * 128 : u * 128 + 128
                    ]
            return carry

        lax.fori_loop(first, last, step, 0)

    def rs_copy(p, i, src, dst, where):
        return start(remote(src, dst, rs_sem.at[0, p, i], rs_sem.at[1, p, i], where))

    def to_sibling(p):
        rows = pl.ds(p * PIECE, PIECE)
        return rs_copy(p, 0, part.at[1 - c, :, rows, :], rc.at[:, rows, :], sib)

    def add(*terms):
        total = terms[0].astype(F32)
        for term in terms[1:]:
            total = total + term.astype(F32)
        return total.astype(BF16)

    def reduce_first(p, core):
        core.wait_recv()
        rows, half = pl.ds(p * PIECE, PIECE), pl.ds(p * HALF, HALF)
        low, high = pl.ds(p * PIECE, HALF), pl.ds(p * PIECE + HALF, HALF)
        out = {}
        for i, j in enumerate((y2, y1, y3, y)):
            part[c, j, rows, :] = add(part[c, j, rows, :], rc[j, rows, :])
            if i == 0:
                out["a0"] = rs_copy(p, 1, part.at[c, j, low, :], a1.at[0, half, :], at_y1)
                out["b0"] = rs_copy(p, 2, part.at[c, j, high, :], b1.at[0, half, :], at_y3)
            elif i == 1:
                out["a1"] = rs_copy(p, 3, part.at[c, j, low, :], a1.at[1, half, :], at_y1)
            elif i == 2:
                out["b1"] = rs_copy(p, 4, part.at[c, j, high, :], b1.at[1, half, :], at_y3)
        return out

    def reduce_second(p, copies):
        half = pl.ds(p * HALF, HALF)
        low, high = pl.ds(p * PIECE, HALF), pl.ds(p * PIECE + HALF, HALF)
        copies["a0"].wait_recv()
        ta[half, :] = add(part[c, y3, low, :], a1[0, half, :])
        copies["a2"] = rs_copy(p, 5, ta.at[half, :], a2.at[half, :], at_y3)
        copies["b0"].wait_recv()
        tb[half, :] = add(part[c, y1, high, :], b1[0, half, :])
        copies["b2"] = rs_copy(p, 6, tb.at[half, :], b2.at[half, :], at_y1)

    def ar_copy(p, i, src, dst, where):
        return start(remote(src, dst, ar_sem.at[0, p, i], ar_sem.at[1, p, i], where))

    def wait_all(copies):
        for copy in copies:
            copy.wait_recv()

    def ar_x_send(p, copies):
        half = pl.ds(p * HALF, HALF)
        low, high = pl.ds(p * PIECE, HALF), pl.ds(p * PIECE + HALF, HALF)
        wait_all([copies["a1"], copies["a2"]])
        gsum[low, :] = add(part[c, y, low, :], a1[1, half, :], a2[half, :])
        wait_all([copies["b1"], copies["b2"]])
        gsum[high, :] = add(part[c, y, high, :], b1[1, half, :], b2[half, :])
        return [
            ar_copy(
                p,
                j - 1,
                gsum.at[pl.ds(p * PIECE + (x + j) % NX * QUARTER, QUARTER), :],
                rx.at[j - 1, pl.ds(p * QUARTER, QUARTER), :],
                at_x[j],
            )
            for j in range(1, NX)
        ]

    def ar_z_send(p, copies):
        wait_all(copies)
        here = pl.ds(p * QUARTER, QUARTER)
        xs[here, :] = add(
            gsum[pl.ds(p * PIECE + x * QUARTER, QUARTER), :], *[rx[j, here, :] for j in range(3)]
        )
        return [
            ar_copy(
                p,
                2 + j,
                xs.at[pl.ds(p * QUARTER + (z + j) % NZ * SHARE, SHARE), :],
                rz.at[j - 1, pl.ds(p * SHARE, SHARE), :],
                at_z[j],
            )
            for j in range(1, NZ)
        ]

    def ar_z_gather(p, copies):
        wait_all(copies)
        here = pl.ds(p * PIECE + x * QUARTER + z * SHARE, SHARE)
        full[here, :] = add(
            xs[pl.ds(p * QUARTER + z * SHARE, SHARE), :],
            *[rz[j, pl.ds(p * SHARE, SHARE), :] for j in range(7)],
        )
        return [
            ar_copy(p, 9 + j, full.at[here, :], full.at[here, :], at_z[j]) for j in range(1, NZ)
        ]

    def ar_x_gather(p, copies):
        wait_all(copies)
        here = pl.ds(p * PIECE + x * QUARTER, QUARTER)
        return [
            ar_copy(p, 16 + j, full.at[here, :], full.at[here, :], at_x[j]) for j in range(1, NX)
        ]

    def v_copy(i, src, dst, where):
        return start(remote(src, dst, v_sem.at[0, i], v_sem.at[1, i], where))

    def v_pair(i, where):
        return v_copy(i, vs.at[i], vr.at[i], where)

    def v_next(i, copy):
        copy.wait_recv()
        vs[i + 1] = vs[i] + vr[i]

    def v_x_send():
        vx[x] = vs[3]
        return [v_copy(2 + j, vs.at[3], vx.at[x], at_x[j]) for j in range(1, NX)]

    def v_z_send(copies):
        for copy in copies:
            copy.wait_recv()
        total = vx[0] + vx[1] + vx[2] + vx[3]
        vs[4] = total
        vz[z] = total
        return [v_copy(5 + j, vs.at[4], vz.at[z], at_z[j]) for j in range(1, NZ)]

    def v_last(copies):
        for copy in copies:
            copy.wait_recv()
        total = vz[0]
        for j in range(1, NZ):
            total = total + vz[j]
        sums_ref[...] = total

    def norm_gradient(slot):
        rows = slice(slot * SLOT, slot * SLOT + SLOT)
        nrm[rows, :] = nt(dqkv[rows, 0 : 3 * WIDTH], wf[...]).astype(BF16)

    def input_gradient(slot):
        def piece(i, carry):
            gsum_, bsum_, qsum_ = carry
            rows = pl.ds(pl.multiple_of(slot * SLOT + i * 32, 32), 32)
            dn = nrm[rows, :].astype(F32)
            h = xh[rows, :]
            gsum_ = gsum_ + jnp.sum(dn * h, axis=0, keepdims=True)
            bsum_ = bsum_ + jnp.sum(dn, axis=0, keepdims=True)
            qsum_ = qsum_ + jnp.sum(dqkv[rows, 0 : 3 * WIDTH].astype(F32), axis=0, keepdims=True)
            d = dn * g_ref[...].reshape(1, -1)
            m1 = jnp.mean(d, axis=-1, keepdims=True)
            m2 = jnp.mean(d * h, axis=-1, keepdims=True)
            pg_ref[rows, :] = (rs[rows, 0:1] * (d - m1 - h * m2)).astype(BF16)
            return gsum_, bsum_, qsum_

        zero = (jnp.zeros((1, 1152), F32), jnp.zeros((1, 1152), F32), jnp.zeros((1, 1728), F32))
        sums = lax.fori_loop(0, 8, piece, zero)
        for first, value in zip((0, 1152, 2304), sums):
            cols = slice(first, first + value.shape[1])
            vs[0, :, cols] = value if slot == 0 else vs[0, :, cols] + value
        if slot == 0:
            vs[0, :, 4032:4096] = jnp.zeros((1, 64), F32)

    def go(advance, slot, k):
        for i in range(NC // 2):
            advance(slot * (NC // 2) + i, k)

    def spread(events):
        events = list(events)

        def after(head):
            for event in events[head * len(events) // HEADS : (head + 1) * len(events) // HEADS]:
                event[0](*event[1:])

        return after

    def steps(advance, slot, k):
        return [(advance, slot * (NC // 2) + i, k) for i in range(NC // 2)]

    for par in range(2):
        for j in range(NY):
            part[par, j, pl.ds(2016, 32), :] = jnp.zeros((32, 128), BF16)
    dqkv[:, 3 * WIDTH :] = jnp.zeros((2 * SLOT, 64), BF16)
    load_x.wait()
    norm(0)
    norm(1)
    go(advance1, 0, 0)
    relays = ag_relay()
    go(advance1, 1, 0)
    transpose()
    go(advance1, 0, 1)
    go(advance1, 1, 1)
    ag_second()
    go(advance1, 0, 2)
    go(advance1, 1, 2)
    go(advance1, 0, 3)
    go(advance1, 1, 3)
    ag_third(relays)
    project(0)
    go(advance1, 0, 4)
    go(advance1, 1, 4)
    project(1)
    forward(0, spread([]))
    go(advance1, 0, 5)
    for i in range(NC // 2):
        send2(i, 0)
    forward(1, spread([]))
    for i in range(NC // 2):
        send2(NC // 2 + i, 0)
    backward(0, spread(steps(advance1, 1, 5) + steps(advance2, 0, 0)))
    backward(1, spread(steps(advance2, 1, 0)))
    early = len(pending)
    core, moving = [], {}
    for p, (first, last) in enumerate(((0, 2), (2, 4), (4, 6), (6, 7))):
        weight_tiles(first, last)
        core.append(to_sibling(p))
        if p == 1:
            go(advance2, 0, 1)
    store_ao = []

    def stage(s, p):
        if s == 1:
            moving[p] = reduce_first(p, core[p])
        elif s == 2:
            reduce_second(p, moving[p])
        else:
            moving[p] = (ar_x_send, ar_z_send, ar_z_gather, ar_x_gather)[s - 3](p, moving[p])

    def store(slot):
        go(advance2, slot, 5)
        copy = pltpu.make_async_copy(
            ao_ref.at[slot], ao_hbm.at[:, pl.ds(slot * SLOT, SLOT)], io_sem.at[1 + slot]
        )
        copy.start()
        store_ao.append(copy)

    stage(1, 0)
    stage(1, 1)
    go(advance2, 1, 1)
    norm_gradient(0)
    go(advance2, 0, 2)
    stage(2, 0)
    stage(1, 2)
    go(advance2, 1, 2)
    input_gradient(0)
    stage(2, 1)
    stage(1, 3)
    go(advance2, 0, 3)
    stage(3, 0)
    norm_gradient(1)
    go(advance2, 1, 3)
    stage(2, 2)
    stage(3, 1)
    stage(4, 0)
    go(advance2, 0, 4)
    input_gradient(1)
    store_pg = pltpu.make_async_copy(pg_ref, pg_hbm, io_sem.at[0])
    store_pg.start()
    va = v_pair(0, sib)
    stage(2, 3)
    stage(3, 2)
    go(advance2, 1, 4)
    stage(4, 1)
    stage(5, 0)
    drain(early)
    v_next(0, va)
    va = v_pair(1, at_y1)
    middle = len(pending)
    store(0)
    stage(3, 3)
    stage(4, 2)
    stage(5, 1)
    stage(6, 0)
    store(1)
    v_next(1, va)
    va = v_pair(2, at_y3)
    stage(4, 3)
    stage(5, 2)
    stage(6, 1)
    v_next(2, va)
    vc = v_x_send()
    drain(middle)
    stage(5, 3)
    stage(6, 2)
    vc = v_z_send(vc)
    late = len(pending)
    stage(6, 3)
    v_last(vc)
    drain(late)
    store_pg.wait()
    for copy in store_ao:
        copy.wait()
    for p in range(PIECES):
        wait_all(moving[p])
    drain(len(pending))


def finish(
    ao_in,
    pg_in,
    full_in,
    sums,
    ao_out,
    pg_out,
    wg_out,
    gg_ref,
    bg_ref,
    qg_ref,
    ao,
    pg,
    full,
    wg,
    in_sem,
    out_sem,
):
    half = pg_in.shape[0] // 2
    part = wg.shape[0] // 3
    load_full = pltpu.make_async_copy(full_in, full, in_sem.at[3])
    pieces = [
        (ref_in.at[rows, :], ref.at[rows, :], ref_out.at[rows, :])
        for ref_in, ref, ref_out, rows in (
            (pg_in, pg, pg_out, pl.ds(0, half)),
            (pg_in, pg, pg_out, pl.ds(half, half)),
            (ao_in, ao, ao_out, pl.ds(0, WIDTH)),
        )
    ]
    loads = [
        pltpu.make_async_copy(src, mid, in_sem.at[i]) for i, (src, mid, _) in enumerate(pieces)
    ]
    stores = [
        pltpu.make_async_copy(mid, dst, out_sem.at[i]) for i, (_, mid, dst) in enumerate(pieces)
    ]
    load_full.start()
    for load in loads:
        load.start()
    load_full.wait()
    for i in range(3):
        for t in range(14):
            wide = min(128, 3 * WIDTH - t * 128)
            wg[i * part : (i + 1) * part, t * 128 : t * 128 + wide] = full[
                pl.ds(t * 144 + i * part, part), 0:wide
            ].astype(F32)
        rows = pl.ds(i * part, part)
        store = pltpu.make_async_copy(wg.at[rows, :], wg_out.at[rows, :], out_sem.at[3 + i])
        store.start()
        stores.append(store)
        loads[i].wait()
        stores[i].start()
    gg_ref[...] = sums[0, 0:1152]
    bg_ref[...] = sums[0, 1152:2304]
    qg_ref[...] = sums[0, 2304:4032]
    for store in stores:
        store.wait()


def body(patches, layer_norm_gain, layer_norm_bias, w_qkv, qkv_bias, out_grad, lengths, target):
    rows, depth = patches.shape
    cols = w_qkv.shape[1]
    full_rows = 8 * w_qkv.shape[0]
    vmem = pl.BlockSpec(memory_space=pltpu.VMEM)
    smem = pl.BlockSpec(memory_space=pltpu.SMEM)
    hbm = pl.BlockSpec(memory_space=pl.ANY)
    shape = jax.ShapeDtypeStruct
    parts = pl.pallas_call(
        kernel,
        out_shape=(
            shape((WIDTH, rows), BF16),
            shape((rows, depth), BF16),
            shape((2048, 128), BF16),
            shape((1, 4096), F32),
        ),
        in_specs=[smem, smem, hbm, vmem, vmem, hbm, vmem, hbm],
        out_specs=[hbm, hbm, vmem, vmem],
        scratch_shapes=[
            pltpu.VMEM((rows, depth), BF16),
            pltpu.VMEM((WIDTH, rows), BF16),
            pltpu.VMEM((2, WIDTH, SLOT), BF16),
            pltpu.VMEM((rows, depth), BF16),
            pltpu.VMEM((full_rows, cols), BF16),
            pltpu.VMEM((rows, depth), F32),
            pltpu.VMEM((rows, depth), BF16),
            pltpu.VMEM((depth, rows), BF16),
            pltpu.VMEM((rows, 128), F32),
            pltpu.VMEM((rows, cols), BF16),
            pltpu.VMEM((rows, WIDTH), BF16),
            pltpu.VMEM((2 * HEADS, SLOT, SLOT), F32),
            pltpu.VMEM((2, WIDTH, SLOT), BF16),
            pltpu.VMEM((rows, cols + 64), BF16),
            pltpu.VMEM((2, WIDTH, SLOT), BF16),
            pltpu.VMEM((5, 2, WIDTH, SLOT), BF16),
            pltpu.VMEM((6, 2, WIDTH, SLOT), BF16),
            pltpu.VMEM((5, 2, WIDTH, SLOT), BF16),
            pltpu.VMEM((6, 2, WIDTH, SLOT), BF16),
            pltpu.VMEM((2, NY, 2048, 128), BF16),
            pltpu.VMEM((NY, 2048, 128), BF16),
            pltpu.VMEM((2, 1024, 128), BF16),
            pltpu.VMEM((2, 1024, 128), BF16),
            pltpu.VMEM((1024, 128), BF16),
            pltpu.VMEM((1024, 128), BF16),
            pltpu.VMEM((1024, 128), BF16),
            pltpu.VMEM((1024, 128), BF16),
            pltpu.VMEM((2048, 128), BF16),
            pltpu.VMEM((3, 512, 128), BF16),
            pltpu.VMEM((512, 128), BF16),
            pltpu.VMEM((7, 64, 128), BF16),
            pltpu.VMEM((5, 1, 4096), F32),
            pltpu.VMEM((3, 1, 4096), F32),
            pltpu.VMEM((NX, 1, 4096), F32),
            pltpu.VMEM((NZ, 1, 4096), F32),
            pltpu.SemaphoreType.DMA((2, 2, NC, HOPS)),
            pltpu.SemaphoreType.DMA((2, 13)),
            pltpu.SemaphoreType.DMA((2, PIECES, 7)),
            pltpu.SemaphoreType.DMA((2, PIECES, 20)),
            pltpu.SemaphoreType.DMA((2, 13)),
            pltpu.SemaphoreType.DMA((3,)),
        ],
        compiler_params=pltpu.CompilerParams(
            collective_id=0, has_side_effects=True, vmem_limit_bytes=58 * 1024 * 1024
        ),
    )(
        lengths,
        target,
        patches,
        layer_norm_gain,
        layer_norm_bias,
        w_qkv,
        qkv_bias,
        out_grad.T,
    )
    out = pl.pallas_call(
        finish,
        out_shape=(
            shape((WIDTH, rows), BF16),
            shape((rows, depth), BF16),
            shape(w_qkv.shape, F32),
            shape((depth,), F32),
            shape((depth,), F32),
            shape((cols,), F32),
        ),
        in_specs=[hbm, hbm, hbm, vmem],
        out_specs=[hbm, hbm, hbm, vmem, vmem, vmem],
        scratch_shapes=[
            pltpu.VMEM((WIDTH, rows), BF16),
            pltpu.VMEM((rows, depth), BF16),
            pltpu.VMEM((2048, 128), BF16),
            pltpu.VMEM(w_qkv.shape, F32),
            pltpu.SemaphoreType.DMA((4,)),
            pltpu.SemaphoreType.DMA((6,)),
        ],
    )(*parts)
    attn_out, patch_gradient, weight_grad, gain, bias, qbias = out
    return attn_out.T, patch_gradient, weight_grad, gain, bias, qbias


def solution(mesh):
    return jax.shard_map(
        body,
        mesh=mesh,
        in_specs=(
            P(("dp", "fsdp"), None),
            P(),
            P(),
            P("fsdp", None),
            P(),
            P(("dp", "fsdp"), None),
            P(("dp", "fsdp")),
            P(("dp", "fsdp")),
        ),
        out_specs=(
            P(("dp", "fsdp"), None),
            P(("dp", "fsdp"), None),
            P("fsdp", None),
            P(),
            P(),
            P(),
        ),
        check_vma=False,
    )
```

```python
import jax
import jax.numpy as jnp
from jax import lax
from jax.experimental import pallas as pl
from jax.experimental.pallas import tpu as pltpu
from jax.sharding import PartitionSpec as P

HEADS = 8
HD = 72
WIDTH = HEADS * HD
SLOT = 256
NX, NZ, NY = 4, 8, 4
F32 = jnp.float32
BF16 = jnp.bfloat16
SCALE = 1.0 / HD**0.5

SWAPS = (
    (
        (-16711936, -16776961),
        (1717960704, -1717960705),
        (-65536, -1),
        (1717960704, -1717960705),
    ),
    (
        (1717960704, -1717960705),
        (-256, -1),
        (1717960704, -1717960705),
        (-16777216, -16776961),
    ),
)
CHUNK = WIDTH // 6


def chunk_steps(i):
    net = i % 2
    steps = [("z", net, s) for s in range(4)]
    first, second = (("x", 1), ("x", 3)) if i // 2 % 2 == 0 else (("x", 3), ("x", 1))
    at = i % 3
    steps.insert(at, first)
    steps.insert(at + 3, second)
    return tuple(steps)


ROUTE = [(slot, i * CHUNK, CHUNK, chunk_steps(i)) for slot in range(2) for i in range(6)]
ROUTE2 = [
    (slot, i * 2 * CHUNK, 2 * CHUNK, chunk_steps(i + 3 * slot)) for slot in range(2) for i in range(3)
]
HOPS = 6
NC = len(ROUTE)
HALF_A = 80
PIECES = 4
PIECE = 2048 // PIECES
HALF, QUARTER, SHARE = PIECE // 2, PIECE // NX, PIECE // NX // NZ


def window(head):
    low = head * HD // 128 * 128
    return low, min((head * HD + HD + 127) // 128 * 128, WIDTH)


def nt(a, b):
    return lax.dot_general(a, b, (((1,), (1,)), ((), ())), preferred_element_type=F32)


def nn(a, b):
    return jnp.dot(a, b, preferred_element_type=F32)


def tn(a, b):
    return lax.dot_general(a, b, (((0,), (0,)), ((), ())), preferred_element_type=F32)


def kernel(
    len_ref,
    tgt_ref,
    x_hbm,
    g_ref,
    b_ref,
    w_hbm,
    qb_ref,
    og_hbm,
    ao_hbm,
    pg_hbm,
    full,
    sums_ref,
    x_ref,
    og_ref,
    ao_ref,
    pg_ref,
    wf,
    xh,
    nrm,
    nrmt,
    rs,
    qkv,
    ks,
    probs,
    do,
    dqkv,
    o,
    s1,
    r1,
    s2,
    r2,
    part,
    rc,
    a1,
    b1,
    a2,
    b2,
    ta,
    tb,
    gsum,
    rx,
    xs,
    rz,
    vs,
    vr,
    vx,
    vz,
    route_sem,
    ag_sem,
    rs_sem,
    ar_sem,
    v_sem,
    io_sem,
):
    dp = lax.axis_index("dp")
    fs = lax.axis_index("fsdp")
    z, x = dp // NX, dp % NX
    y, c = fs // 2, fs % 2
    even = (z + 1 - 2 * (z % 2)) * NX + x
    odd = (z + NZ - 1 + 2 * (z % 2)) % NZ * NX + x
    partner = {("x", 1): z * NX + (x + 1 - 2 * (x % 2)), ("x", 3): z * NX + (3 - x)}
    for net in range(2):
        for stage in range(4):
            partner["z", net, stage] = odd if (net + stage) % 2 else even
    y1, y2, y3 = y + 1 - 2 * (y % 2), (y + 2) % NY, 3 - y
    sib = (dp, y * 2 + 1 - c)
    at_y1 = (dp, y1 * 2 + c)
    at_y3 = (dp, y3 * 2 + c)
    at_x = [None] + [(z * NX + (x + j) % NX, fs) for j in range(1, NX)]
    at_z = [None] + [((z + j) % NZ * NX + x, fs) for j in range(1, NZ)]

    def remote(src, dst, send, recv, where):
        return pltpu.make_async_remote_copy(
            src_ref=src,
            dst_ref=dst,
            send_sem=send,
            recv_sem=recv,
            device_id=where,
            device_id_type=pl.DeviceIdType.MESH,
        )

    load_og = pltpu.make_async_copy(og_hbm, og_ref, io_sem.at[0])
    load_w = pltpu.make_async_copy(w_hbm, wf.at[pl.ds(fs * 144, 144), :], io_sem.at[1])
    load_x = pltpu.make_async_copy(x_hbm, x_ref, io_sem.at[2])
    load_w.start()
    load_og.start()
    load_x.start()
    barrier = pltpu.get_barrier_semaphore()
    peers = [sib, at_y1, at_y3] + at_x[1:] + at_z[1:]
    for peer in peers:
        pl.semaphore_signal(barrier, inc=1, device_id=peer, device_id_type=pl.DeviceIdType.MESH)
    load_w.wait()
    load_og.wait()
    pl.semaphore_wait(barrier, len(peers))

    pending = []

    def start(copy):
        copy.start()
        pending.append(copy)
        return copy

    def drain(count):
        for copy in pending[:count]:
            copy.wait_send()
        del pending[:count]

    flip = []
    for slot in range(2):
        mask = jnp.bitwise_xor(tgt_ref[slot], dp)
        bits = [jnp.bitwise_and(jnp.right_shift(mask, i), 1) for i in range(2)]
        zmask = jnp.right_shift(mask, 2)
        shift = jnp.bitwise_and(zmask, 3) * 8 + z
        swap = {
            ("x", 1): jnp.bitwise_xor(bits[0], bits[1]) == 1,
            ("x", 3): bits[1] == 1,
        }
        for net in range(2):
            for stage in range(4):
                low, high = SWAPS[net][stage]
                word = jnp.where(zmask < 4, jnp.int32(low), jnp.int32(high))
                swap["z", net, stage] = jnp.bitwise_and(jnp.right_shift(word, shift), 1) == 1
        flip.append(swap)

    def route(which, plan, first, sbuf, rbuf, last):
        def place(ref, i):
            slot, row, rows, _ = plan[i]
            if len(ref.shape) == 2:
                return ref.at[pl.ds(row, rows), pl.ds(slot * SLOT, SLOT)]
            return ref.at[slot, pl.ds(row, rows), :]

        def source(i, k):
            return place(first if k == 0 else sbuf.at[k - 1], i)

        copies = {}

        def send(i, k):
            order = plan[i][3]
            copies[i, k] = start(
                remote(
                    source(i, k),
                    place(rbuf.at[k], i),
                    route_sem.at[which, 0, i, k],
                    route_sem.at[which, 1, i, k],
                    (partner[order[k]], fs),
                )
            )

        def advance(i, k):
            slot, _, _, order = plan[i]
            copies[i, k].wait_recv()
            value = jnp.where(
                flip[slot][order[k]], place(rbuf.at[k], i)[...], source(i, k)[...]
            )
            if k < HOPS - 1:
                place(sbuf.at[k], i)[...] = value
                send(i, k + 1)
            else:
                place(last, i)[...] = value

        advance.half = len(plan) // 2
        return send, advance

    send1, advance1 = route(0, ROUTE, og_ref, s1, r1, do)
    send2, advance2 = route(1, ROUTE2, o, s2, r2, ao_ref)

    def ag(i, src, row, rows, where):
        return start(
            remote(src, wf.at[pl.ds(row, rows), :], ag_sem.at[0, i], ag_sem.at[1, i], where)
        )

    rest = 144 - HALF_A
    own = fs * 144
    row1, row2, row3 = (y1 * 2 + c) * 144, (y2 * 2 + c) * 144, (y3 * 2 + c) * 144
    head_rows, tail_rows = wf.at[pl.ds(own, HALF_A), :], wf.at[pl.ds(own + HALF_A, rest), :]

    def rows_of(row, rows):
        return wf.at[pl.ds(row, rows), :]

    ag_a0 = ag(0, head_rows, own, HALF_A, at_y1)
    ag_b0 = ag(1, tail_rows, own + HALF_A, rest, at_y3)
    for i in range(NC):
        send1(i, 0)
    ag_a1 = ag(2, tail_rows, own + HALF_A, rest, at_y1)
    ag_b1 = ag(3, head_rows, own, HALF_A, at_y3)
    to_sib = [ag(4, wf.at[pl.ds(own, 144), :], own, 144, sib)]

    def ag_relay():
        ag_a0.wait_recv()
        relay_a = ag(5, rows_of(row1, HALF_A), row1, HALF_A, at_y3)
        to_sib.append(ag(7, rows_of(row1, HALF_A), row1, HALF_A, sib))
        ag_b0.wait_recv()
        relay_b = ag(6, rows_of(row3 + HALF_A, rest), row3 + HALF_A, rest, at_y1)
        to_sib.append(ag(8, rows_of(row3 + HALF_A, rest), row3 + HALF_A, rest, sib))
        return relay_a, relay_b

    def ag_second():
        ag_a1.wait_recv()
        to_sib.append(ag(9, rows_of(row1 + HALF_A, rest), row1 + HALF_A, rest, sib))
        ag_b1.wait_recv()
        to_sib.append(ag(10, rows_of(row3, HALF_A), row3, HALF_A, sib))

    def ag_third(relays):
        relays[0].wait_recv()
        to_sib.append(ag(11, rows_of(row2, HALF_A), row2, HALF_A, sib))
        relays[1].wait_recv()
        to_sib.append(ag(12, rows_of(row2 + HALF_A, rest), row2 + HALF_A, rest, sib))
        for copy in to_sib:
            copy.wait_recv()

    def norm(slot):
        def step(i, _):
            rows = pl.ds(pl.multiple_of(slot * SLOT + i * 32, 32), 32)
            v = x_ref[rows, :].astype(F32)
            v = v - jnp.mean(v, axis=-1, keepdims=True)
            inv = lax.rsqrt(jnp.mean(v * v, axis=-1, keepdims=True) + 1e-6)
            v = v * inv
            xh[rows, :] = v
            rs[rows, :] = jnp.broadcast_to(inv, (32, 128))
            nrm[rows, :] = (v * g_ref[...].reshape(1, -1) + b_ref[...].reshape(1, -1)).astype(BF16)
            return 0

        lax.fori_loop(0, SLOT // 32, step, 0)

    def transpose():
        for slot in range(2):
            rows = slice(slot * SLOT, slot * SLOT + SLOT)
            nrmt[:, rows] = nrm[rows, :].T

    def project(slot):
        rows = slice(slot * SLOT, slot * SLOT + SLOT)
        qkv[rows, :] = (nn(nrm[rows, :], wf[...]) + qb_ref[...].reshape(1, -1)).astype(BF16)
        ks[rows, :] = qkv[rows, WIDTH : 2 * WIDTH]

    def lanes(head):
        low, high = window(head)
        lane = lax.broadcasted_iota(jnp.int32, (1, high - low), 1) + low
        inside = (lane >= head * HD) & (lane < head * HD + HD)
        return inside.astype(F32).astype(BF16)

    def tiles_add(store, head, value, axis):
        low, high = window(head)
        for n in range(low, high, 128):
            piece = lax.slice_in_dim(value, n - low, min(n + 128, high) - low, axis=axis)
            store[n] = store[n] + piece if n in store else piece

    def forward(slot, after):
        rows = slice(slot * SLOT, slot * SLOT + SLOT)
        length = len_ref[slot]
        live = lax.broadcasted_iota(jnp.int32, (SLOT, 1), 0) < length
        live_lane = lax.broadcasted_iota(jnp.int32, (1, SLOT), 1) < length
        out = {}
        for head in range(HEADS):
            low, high = window(head)
            mine = lanes(head)
            q = qkv[rows, low:high] * mine
            k = ks[rows, low:high]
            v = qkv[rows, 2 * WIDTH + low : 2 * WIDTH + high] * mine
            s = jnp.where(live, nt(k, q) * SCALE, -1e30)
            e = jnp.exp(s - jnp.max(s, axis=0, keepdims=True))
            p = e / jnp.sum(e, axis=0, keepdims=True)
            probs[slot * HEADS + head] = p
            value = jnp.where(live_lane, tn(v, p.astype(BF16)), 0.0).astype(BF16)
            tiles_add(out, head, value, 0)
            after(head)
        for n, value in out.items():
            o[slot, n : n + value.shape[0], :] = value

    def backward(slot, after):
        rows = slice(slot * SLOT, slot * SLOT + SLOT)
        live_lane = lax.broadcasted_iota(jnp.int32, (1, SLOT), 1) < len_ref[slot]
        gq, gk, gv = {}, {}, {}
        for head in range(HEADS):
            low, high = window(head)
            mine = lanes(head)
            row = lax.broadcasted_iota(jnp.int32, (high - low, 1), 0) + low
            keep = (row >= head * HD) & (row < head * HD + HD) & live_lane
            q = qkv[rows, low:high] * mine
            k = ks[rows, low:high] * mine
            v = qkv[rows, 2 * WIDTH + low : 2 * WIDTH + high]
            up = jnp.where(keep, do[slot, low:high, :].astype(F32), 0.0).astype(BF16)
            p = probs[slot * HEADS + head]
            tiles_add(gv, head, nt(p.astype(BF16), up).astype(BF16), 1)
            gp = nn(v, up)
            delta = jnp.sum(gp * p, axis=0, keepdims=True)
            gs = (p * (gp - delta) * SCALE).astype(BF16)
            tiles_add(gk, head, nn(gs, q).astype(BF16), 1)
            tiles_add(gq, head, tn(gs, k).astype(BF16), 1)
            after(head)
        for n, value in gq.items():
            dqkv[rows, n : n + value.shape[1]] = value
        gk = jnp.concatenate([gk[n] for n in sorted(gk)], axis=1)
        dqkv[rows, WIDTH : 2 * WIDTH] = gk
        for n, value in gv.items():
            dqkv[rows, 2 * WIDTH + n : 2 * WIDTH + n + value.shape[1]] = value

    def weight_tiles(first, last):
        def step(pair, carry):
            cols = pl.ds(pl.multiple_of(pair * 256, 256), 256)
            value = nn(nrmt[...], dqkv[:, cols]).astype(BF16)
            for owner in range(8):
                for u in range(2):
                    row = pl.multiple_of(pair * 288 + u * 144, 16)
                    part[owner % 2, owner // 2, pl.ds(row, 144), :] = value[
                        owner * 144 : owner * 144 + 144, u * 128 : u * 128 + 128
                    ]
            return carry

        lax.fori_loop(first, last, step, 0)

    def rs_copy(p, i, src, dst, where):
        return start(remote(src, dst, rs_sem.at[0, p, i], rs_sem.at[1, p, i], where))

    def to_sibling(p):
        rows = pl.ds(p * PIECE, PIECE)
        return rs_copy(p, 0, part.at[1 - c, :, rows, :], rc.at[:, rows, :], sib)

    def add(*terms):
        total = terms[0].astype(F32)
        for term in terms[1:]:
            total = total + term.astype(F32)
        return total.astype(BF16)

    def reduce_first(p, core):
        core.wait_recv()
        rows, half = pl.ds(p * PIECE, PIECE), pl.ds(p * HALF, HALF)
        low, high = pl.ds(p * PIECE, HALF), pl.ds(p * PIECE + HALF, HALF)
        out = {}
        for i, j in enumerate((y2, y1, y3, y)):
            part[c, j, rows, :] = add(part[c, j, rows, :], rc[j, rows, :])
            if i == 0:
                out["a0"] = rs_copy(p, 1, part.at[c, j, low, :], a1.at[0, half, :], at_y1)
                out["b0"] = rs_copy(p, 2, part.at[c, j, high, :], b1.at[0, half, :], at_y3)
            elif i == 1:
                out["a1"] = rs_copy(p, 3, part.at[c, j, low, :], a1.at[1, half, :], at_y1)
            elif i == 2:
                out["b1"] = rs_copy(p, 4, part.at[c, j, high, :], b1.at[1, half, :], at_y3)
        return out

    def reduce_second(p, copies):
        half = pl.ds(p * HALF, HALF)
        low, high = pl.ds(p * PIECE, HALF), pl.ds(p * PIECE + HALF, HALF)
        copies["a0"].wait_recv()
        ta[half, :] = add(part[c, y3, low, :], a1[0, half, :])
        copies["a2"] = rs_copy(p, 5, ta.at[half, :], a2.at[half, :], at_y3)
        copies["b0"].wait_recv()
        tb[half, :] = add(part[c, y1, high, :], b1[0, half, :])
        copies["b2"] = rs_copy(p, 6, tb.at[half, :], b2.at[half, :], at_y1)

    def ar_copy(p, i, src, dst, where):
        return start(remote(src, dst, ar_sem.at[0, p, i], ar_sem.at[1, p, i], where))

    def wait_all(copies):
        for copy in copies:
            copy.wait_recv()

    def ar_x_send(p, copies):
        half = pl.ds(p * HALF, HALF)
        low, high = pl.ds(p * PIECE, HALF), pl.ds(p * PIECE + HALF, HALF)
        wait_all([copies["a1"], copies["a2"]])
        gsum[low, :] = add(part[c, y, low, :], a1[1, half, :], a2[half, :])
        wait_all([copies["b1"], copies["b2"]])
        gsum[high, :] = add(part[c, y, high, :], b1[1, half, :], b2[half, :])
        return [
            ar_copy(
                p,
                j - 1,
                gsum.at[pl.ds(p * PIECE + (x + j) % NX * QUARTER, QUARTER), :],
                rx.at[j - 1, pl.ds(p * QUARTER, QUARTER), :],
                at_x[j],
            )
            for j in range(1, NX)
        ]

    def ar_z_send(p, copies):
        wait_all(copies)
        here = pl.ds(p * QUARTER, QUARTER)
        xs[here, :] = add(
            gsum[pl.ds(p * PIECE + x * QUARTER, QUARTER), :], *[rx[j, here, :] for j in range(3)]
        )
        return [
            ar_copy(
                p,
                2 + j,
                xs.at[pl.ds(p * QUARTER + (z + j) % NZ * SHARE, SHARE), :],
                rz.at[j - 1, pl.ds(p * SHARE, SHARE), :],
                at_z[j],
            )
            for j in range(1, NZ)
        ]

    def ar_z_gather(p, copies):
        wait_all(copies)
        here = pl.ds(p * PIECE + x * QUARTER + z * SHARE, SHARE)
        full[here, :] = add(
            xs[pl.ds(p * QUARTER + z * SHARE, SHARE), :],
            *[rz[j, pl.ds(p * SHARE, SHARE), :] for j in range(7)],
        )
        return [
            ar_copy(p, 9 + j, full.at[here, :], full.at[here, :], at_z[j]) for j in range(1, NZ)
        ]

    def ar_x_gather(p, copies):
        wait_all(copies)
        here = pl.ds(p * PIECE + x * QUARTER, QUARTER)
        return [
            ar_copy(p, 16 + j, full.at[here, :], full.at[here, :], at_x[j]) for j in range(1, NX)
        ]

    def v_copy(i, src, dst, where):
        return start(remote(src, dst, v_sem.at[0, i], v_sem.at[1, i], where))

    def v_pair(i, where):
        return v_copy(i, vs.at[i], vr.at[i], where)

    def v_next(i, copy):
        copy.wait_recv()
        vs[i + 1] = vs[i] + vr[i]

    def v_x_send():
        vx[x] = vs[3]
        return [v_copy(2 + j, vs.at[3], vx.at[x], at_x[j]) for j in range(1, NX)]

    def v_z_send(copies):
        for copy in copies:
            copy.wait_recv()
        total = vx[0] + vx[1] + vx[2] + vx[3]
        vs[4] = total
        vz[z] = total
        return [v_copy(5 + j, vs.at[4], vz.at[z], at_z[j]) for j in range(1, NZ)]

    def v_last(copies):
        for copy in copies:
            copy.wait_recv()
        total = vz[0]
        for j in range(1, NZ):
            total = total + vz[j]
        sums_ref[...] = total

    def norm_gradient(slot):
        rows = slice(slot * SLOT, slot * SLOT + SLOT)
        nrm[rows, :] = nt(dqkv[rows, 0 : 3 * WIDTH], wf[...]).astype(BF16)

    def input_gradient(slot):
        def piece(i, carry):
            gsum_, bsum_, qsum_ = carry
            rows = pl.ds(pl.multiple_of(slot * SLOT + i * 32, 32), 32)
            dn = nrm[rows, :].astype(F32)
            h = xh[rows, :]
            gsum_ = gsum_ + jnp.sum(dn * h, axis=0, keepdims=True)
            bsum_ = bsum_ + jnp.sum(dn, axis=0, keepdims=True)
            qsum_ = qsum_ + jnp.sum(dqkv[rows, 0 : 3 * WIDTH].astype(F32), axis=0, keepdims=True)
            d = dn * g_ref[...].reshape(1, -1)
            m1 = jnp.mean(d, axis=-1, keepdims=True)
            m2 = jnp.mean(d * h, axis=-1, keepdims=True)
            pg_ref[rows, :] = (rs[rows, 0:1] * (d - m1 - h * m2)).astype(BF16)
            return gsum_, bsum_, qsum_

        zero = (jnp.zeros((1, 1152), F32), jnp.zeros((1, 1152), F32), jnp.zeros((1, 1728), F32))
        sums = lax.fori_loop(0, 8, piece, zero)
        for first, value in zip((0, 1152, 2304), sums):
            cols = slice(first, first + value.shape[1])
            vs[0, :, cols] = value if slot == 0 else vs[0, :, cols] + value
        if slot == 0:
            vs[0, :, 4032:4096] = jnp.zeros((1, 64), F32)

    def go(advance, slot, k):
        for i in range(advance.half):
            advance(slot * advance.half + i, k)

    def spread(events):
        events = list(events)

        def after(head):
            for event in events[head * len(events) // HEADS : (head + 1) * len(events) // HEADS]:
                event[0](*event[1:])

        return after

    def steps(advance, slot, k):
        return [(advance, slot * advance.half + i, k) for i in range(advance.half)]

    for par in range(2):
        for j in range(NY):
            part[par, j, pl.ds(2016, 32), :] = jnp.zeros((32, 128), BF16)
    dqkv[:, 3 * WIDTH :] = jnp.zeros((2 * SLOT, 64), BF16)
    load_x.wait()
    norm(0)
    norm(1)
    go(advance1, 0, 0)
    relays = ag_relay()
    go(advance1, 1, 0)
    transpose()
    go(advance1, 0, 1)
    go(advance1, 1, 1)
    ag_second()
    go(advance1, 0, 2)
    go(advance1, 1, 2)
    go(advance1, 0, 3)
    go(advance1, 1, 3)
    ag_third(relays)
    project(0)
    go(advance1, 0, 4)
    go(advance1, 1, 4)
    project(1)
    forward(0, spread([]))
    go(advance1, 0, 5)
    for i in range(3):
        send2(i, 0)
    forward(1, spread([]))
    for i in range(3):
        send2(3 + i, 0)
    backward(0, spread(steps(advance1, 1, 5) + steps(advance2, 0, 0)))
    backward(1, spread(steps(advance2, 1, 0)))
    early = len(pending)
    core, moving = [], {}
    for p, (first, last) in enumerate(((0, 2), (2, 4), (4, 6), (6, 7))):
        weight_tiles(first, last)
        core.append(to_sibling(p))
        if p == 1:
            go(advance2, 0, 1)
    store_ao = []

    def stage(s, p):
        if s == 1:
            moving[p] = reduce_first(p, core[p])
        elif s == 2:
            reduce_second(p, moving[p])
        else:
            moving[p] = (ar_x_send, ar_z_send, ar_z_gather, ar_x_gather)[s - 3](p, moving[p])

    def store(slot):
        go(advance2, slot, 5)
        copy = pltpu.make_async_copy(
            ao_ref.at[slot], ao_hbm.at[:, pl.ds(slot * SLOT, SLOT)], io_sem.at[1 + slot]
        )
        copy.start()
        store_ao.append(copy)

    stage(1, 0)
    stage(1, 1)
    go(advance2, 1, 1)
    norm_gradient(0)
    go(advance2, 0, 2)
    stage(2, 0)
    stage(1, 2)
    go(advance2, 1, 2)
    input_gradient(0)
    stage(2, 1)
    stage(1, 3)
    go(advance2, 0, 3)
    stage(3, 0)
    norm_gradient(1)
    go(advance2, 1, 3)
    stage(2, 2)
    stage(3, 1)
    stage(4, 0)
    go(advance2, 0, 4)
    input_gradient(1)
    store_pg = pltpu.make_async_copy(pg_ref, pg_hbm, io_sem.at[0])
    store_pg.start()
    va = v_pair(0, sib)
    stage(2, 3)
    stage(3, 2)
    go(advance2, 1, 4)
    stage(4, 1)
    stage(5, 0)
    drain(early)
    v_next(0, va)
    va = v_pair(1, at_y1)
    middle = len(pending)
    store(0)
    stage(3, 3)
    stage(4, 2)
    stage(5, 1)
    stage(6, 0)
    store(1)
    v_next(1, va)
    va = v_pair(2, at_y3)
    stage(4, 3)
    stage(5, 2)
    stage(6, 1)
    v_next(2, va)
    vc = v_x_send()
    drain(middle)
    stage(5, 3)
    stage(6, 2)
    vc = v_z_send(vc)
    late = len(pending)
    stage(6, 3)
    v_last(vc)
    drain(late)
    store_pg.wait()
    for copy in store_ao:
        copy.wait()
    for p in range(PIECES):
        wait_all(moving[p])
    drain(len(pending))


def finish(
    ao_in,
    pg_in,
    full_in,
    sums,
    ao_out,
    pg_out,
    wg_out,
    gg_ref,
    bg_ref,
    qg_ref,
    ao,
    pg,
    full,
    wg,
    in_sem,
    out_sem,
):
    half = pg_in.shape[0] // 2
    part = wg.shape[0] // 3
    load_full = pltpu.make_async_copy(full_in, full, in_sem.at[3])
    pieces = [
        (ref_in.at[rows, :], ref.at[rows, :], ref_out.at[rows, :])
        for ref_in, ref, ref_out, rows in (
            (pg_in, pg, pg_out, pl.ds(0, half)),
            (pg_in, pg, pg_out, pl.ds(half, half)),
            (ao_in, ao, ao_out, pl.ds(0, WIDTH)),
        )
    ]
    loads = [
        pltpu.make_async_copy(src, mid, in_sem.at[i]) for i, (src, mid, _) in enumerate(pieces)
    ]
    stores = [
        pltpu.make_async_copy(mid, dst, out_sem.at[i]) for i, (_, mid, dst) in enumerate(pieces)
    ]
    load_full.start()
    for load in loads:
        load.start()
    load_full.wait()
    for i in range(3):
        for t in range(14):
            wide = min(128, 3 * WIDTH - t * 128)
            wg[i * part : (i + 1) * part, t * 128 : t * 128 + wide] = full[
                pl.ds(t * 144 + i * part, part), 0:wide
            ].astype(F32)
        rows = pl.ds(i * part, part)
        store = pltpu.make_async_copy(wg.at[rows, :], wg_out.at[rows, :], out_sem.at[3 + i])
        store.start()
        stores.append(store)
        loads[i].wait()
        stores[i].start()
    gg_ref[...] = sums[0, 0:1152]
    bg_ref[...] = sums[0, 1152:2304]
    qg_ref[...] = sums[0, 2304:4032]
    for store in stores:
        store.wait()


def body(patches, layer_norm_gain, layer_norm_bias, w_qkv, qkv_bias, out_grad, lengths, target):
    rows, depth = patches.shape
    cols = w_qkv.shape[1]
    full_rows = 8 * w_qkv.shape[0]
    vmem = pl.BlockSpec(memory_space=pltpu.VMEM)
    smem = pl.BlockSpec(memory_space=pltpu.SMEM)
    hbm = pl.BlockSpec(memory_space=pl.ANY)
    shape = jax.ShapeDtypeStruct
    parts = pl.pallas_call(
        kernel,
        out_shape=(
            shape((WIDTH, rows), BF16),
            shape((rows, depth), BF16),
            shape((2048, 128), BF16),
            shape((1, 4096), F32),
        ),
        in_specs=[smem, smem, hbm, vmem, vmem, hbm, vmem, hbm],
        out_specs=[hbm, hbm, vmem, vmem],
        scratch_shapes=[
            pltpu.VMEM((rows, depth), BF16),
            pltpu.VMEM((WIDTH, rows), BF16),
            pltpu.VMEM((2, WIDTH, SLOT), BF16),
            pltpu.VMEM((rows, depth), BF16),
            pltpu.VMEM((full_rows, cols), BF16),
            pltpu.VMEM((rows, depth), F32),
            pltpu.VMEM((rows, depth), BF16),
            pltpu.VMEM((depth, rows), BF16),
            pltpu.VMEM((rows, 128), F32),
            pltpu.VMEM((rows, cols), BF16),
            pltpu.VMEM((rows, WIDTH), BF16),
            pltpu.VMEM((2 * HEADS, SLOT, SLOT), F32),
            pltpu.VMEM((2, WIDTH, SLOT), BF16),
            pltpu.VMEM((rows, cols + 64), BF16),
            pltpu.VMEM((2, WIDTH, SLOT), BF16),
            pltpu.VMEM((5, 2, WIDTH, SLOT), BF16),
            pltpu.VMEM((6, 2, WIDTH, SLOT), BF16),
            pltpu.VMEM((5, 2, WIDTH, SLOT), BF16),
            pltpu.VMEM((6, 2, WIDTH, SLOT), BF16),
            pltpu.VMEM((2, NY, 2048, 128), BF16),
            pltpu.VMEM((NY, 2048, 128), BF16),
            pltpu.VMEM((2, 1024, 128), BF16),
            pltpu.VMEM((2, 1024, 128), BF16),
            pltpu.VMEM((1024, 128), BF16),
            pltpu.VMEM((1024, 128), BF16),
            pltpu.VMEM((1024, 128), BF16),
            pltpu.VMEM((1024, 128), BF16),
            pltpu.VMEM((2048, 128), BF16),
            pltpu.VMEM((3, 512, 128), BF16),
            pltpu.VMEM((512, 128), BF16),
            pltpu.VMEM((7, 64, 128), BF16),
            pltpu.VMEM((5, 1, 4096), F32),
            pltpu.VMEM((3, 1, 4096), F32),
            pltpu.VMEM((NX, 1, 4096), F32),
            pltpu.VMEM((NZ, 1, 4096), F32),
            pltpu.SemaphoreType.DMA((2, 2, NC, HOPS)),
            pltpu.SemaphoreType.DMA((2, 13)),
            pltpu.SemaphoreType.DMA((2, PIECES, 7)),
            pltpu.SemaphoreType.DMA((2, PIECES, 20)),
            pltpu.SemaphoreType.DMA((2, 13)),
            pltpu.SemaphoreType.DMA((3,)),
        ],
        compiler_params=pltpu.CompilerParams(
            collective_id=0, has_side_effects=True, vmem_limit_bytes=58 * 1024 * 1024
        ),
    )(
        lengths,
        target,
        patches,
        layer_norm_gain,
        layer_norm_bias,
        w_qkv,
        qkv_bias,
        out_grad.T,
    )
    out = pl.pallas_call(
        finish,
        out_shape=(
            shape((WIDTH, rows), BF16),
            shape((rows, depth), BF16),
            shape(w_qkv.shape, F32),
            shape((depth,), F32),
            shape((depth,), F32),
            shape((cols,), F32),
        ),
        in_specs=[hbm, hbm, hbm, vmem],
        out_specs=[hbm, hbm, hbm, vmem, vmem, vmem],
        scratch_shapes=[
            pltpu.VMEM((WIDTH, rows), BF16),
            pltpu.VMEM((rows, depth), BF16),
            pltpu.VMEM((2048, 128), BF16),
            pltpu.VMEM(w_qkv.shape, F32),
            pltpu.SemaphoreType.DMA((4,)),
            pltpu.SemaphoreType.DMA((6,)),
        ],
    )(*parts)
    attn_out, patch_gradient, weight_grad, gain, bias, qbias = out
    return attn_out.T, patch_gradient, weight_grad, gain, bias, qbias


def solution(mesh):
    return jax.shard_map(
        body,
        mesh=mesh,
        in_specs=(
            P(("dp", "fsdp"), None),
            P(),
            P(),
            P("fsdp", None),
            P(),
            P(("dp", "fsdp"), None),
            P(("dp", "fsdp")),
            P(("dp", "fsdp")),
        ),
        out_specs=(
            P(("dp", "fsdp"), None),
            P(("dp", "fsdp"), None),
            P("fsdp", None),
            P(),
            P(),
            P(),
        ),
        check_vma=False,
    )
```
